256 devices in a mesh: stn: 64 (over z_hi, x, y), beam: 4 (over z_lo, core).
Axes of the slice: x: 4, y: 4, z: 8 (z_hi: 4, z_lo: 2; z = z_hi * 2 + z_lo), core: 2. Of those that a mesh axis runs over, the one named last changes fastest.
Arguments:
- voltages: bfloat16 [2, 1024, 131072], P(None, 'stn', 'beam'), may hold values from -6 to 6
- filter_taps: float32 [12, 128], replicated, may hold values from -1.8 to 1.8
- synth_taps: float32 [12, 128], replicated, may hold values from -1.8 to 1.8
- beam_weights: bfloat16 [2, 128, 512, 1024], P(None, 'stn', 'beam'), may hold values from -0.125 to 0.125
- station_order: int32 [1024], replicated, may hold values from 0 to 1023, each once
Outputs:
- visibilities: float32 [2, 128, 1024, 1024], P(None, 'stn', 'beam')
- beam_series: float32 [2, 4, 128, 131072], P(None, 'beam', 'stn')
The draws below stay inside these ranges and needn't reach their ends.
Inputs may be any that keep to these rules, and one draw needn't show every extreme that they name: `station_order`: a permutation of the 1024 station numbers.
All inputs are finite; a program needn't handle non-finite values.
Results may differ from the reference program's by a relative error of at most 0.0029.
Values may be sent and summed in bfloat16 or wider, within the bound.
A program may use at most 128 MiB of HBM per device.

```python
import math
import jax
import jax.numpy as jnp
from jax import lax

CHANNELS = 128
TAPS = 12
BEAMS = 512
STATIONS = 1024
SPECTRA = 1024
SAMPLES = 131072
GROUP_BEAMS = 128
N_BEAM = 4


def shard_levels(stream_key, dims, cuts, least, top_value):
    loudness, own = 1.0, jax.random.fold_in(stream_key, 6)
    for dim, shards_of in cuts:
        heights = jnp.exp(jax.random.uniform(jax.random.fold_in(own, dim), (shards_of,), jnp.float32, least / len(cuts), top_value / len(cuts)))
        loudness = loudness * jnp.repeat(heights, dims[dim] // shards_of).reshape([-1 if axis == dim else 1 for axis in range(len(dims))])
    return loudness


def centred(stream_key, dims, deviation, limit, pieces=(), kind=jnp.bfloat16):
    entries = deviation * jax.random.normal(stream_key, dims, jnp.float32)
    if pieces:
        entries = entries * shard_levels(stream_key, dims, pieces, -0.22, 0.18)
    return jnp.clip(entries, -limit, limit).astype(kind)


def setup_inputs(seed: int = 0) -> dict:
    key_list = jax.random.split(jax.random.key(seed), 6)
    voltages = centred(key_list[0], (2, STATIONS, SAMPLES), 1.0, 6.0, ((1, 64), (2, 4)))
    filter_taps = centred(key_list[1], (TAPS, CHANNELS), 0.3, 1.8, (), jnp.float32)
    synth_taps = centred(key_list[2], (TAPS, CHANNELS), 0.3, 1.8, (), jnp.float32)
    beam_weights = centred(key_list[3], (2, CHANNELS, BEAMS, STATIONS), (2 * STATIONS) ** -0.5, 0.125, ((1, 64), (2, 4)))
    station_order = jax.random.permutation(key_list[4], STATIONS).astype(jnp.int32)
    return {"voltages": voltages, "filter_taps": filter_taps, "synth_taps": synth_taps, "beam_weights": beam_weights, "station_order": station_order}


def spin_matrix(points):
    positions = jnp.arange(points, dtype=jnp.int32)
    phase_idx = positions[:, None] * positions[None, :] % points
    angles = phase_idx.astype(jnp.float32) * (2.0 * math.pi / points)
    cosine = jnp.cos(angles) / math.sqrt(points)
    sine_part = jnp.sin(angles) / math.sqrt(points)
    upper_half = jnp.concatenate([cosine, -sine_part], axis=1)
    lower_half = jnp.concatenate([sine_part, cosine], axis=1)
    return jnp.concatenate([upper_half, lower_half], axis=0)

def correlate(channel_block):
    real_part = channel_block[0].astype(jnp.float32)
    imag_part = channel_block[1].astype(jnp.float32)
    joined = jnp.concatenate([real_part, imag_part], axis=1)
    turned = jnp.concatenate([imag_part, -real_part], axis=1)
    real_sum = jnp.dot(joined, joined.T, precision=lax.Precision.HIGHEST, preferred_element_type=jnp.float32)
    imag_sum = jnp.dot(turned, joined.T, precision=lax.Precision.HIGHEST, preferred_element_type=jnp.float32)
    return jnp.stack([real_sum, imag_sum]) / SPECTRA

def form_beams(operands):
    channel_block, weight = operands
    real_part = channel_block[0].astype(jnp.float32)
    imag_part = channel_block[1].astype(jnp.float32)
    weight_real = weight[0].astype(jnp.float32)
    weight_imag = weight[1].astype(jnp.float32)
    weight_wide = jnp.concatenate([jnp.concatenate([weight_real, -weight_imag], axis=1), jnp.concatenate([weight_imag, weight_real], axis=1)], axis=0)
    stacked = jnp.concatenate([real_part, imag_part], axis=0)
    return jnp.dot(weight_wide, stacked, precision=lax.Precision.HIGHEST, preferred_element_type=jnp.float32)

def reference(voltages, filter_taps, synth_taps, beam_weights, station_order):
    matrix = spin_matrix(CHANNELS)
    samples = voltages.astype(jnp.float32).reshape(2, STATIONS, SPECTRA, CHANNELS)
    padded = jnp.pad(samples, ((0, 0), (0, 0), (TAPS - 1, 0), (0, 0)))
    windowed = jnp.zeros_like(samples)
    for tap_index in range(TAPS):
        begin_at = TAPS - 1 - tap_index
        windowed = windowed + filter_taps[tap_index] * padded[:, :, begin_at:begin_at + SPECTRA, :]
    flattened = jnp.concatenate([windowed[0], windowed[1]], axis=-1).reshape(STATIONS * SPECTRA, 2 * CHANNELS)
    spectra_rows = jnp.dot(flattened, matrix, precision=lax.Precision.HIGHEST, preferred_element_type=jnp.float32).astype(jnp.bfloat16)
    spectra_rows = spectra_rows.reshape(STATIONS, SPECTRA, 2, CHANNELS)
    inverse = jnp.zeros((STATIONS,), jnp.int32).at[station_order].set(jnp.arange(STATIONS, dtype=jnp.int32))
    spectra = spectra_rows[inverse]
    channel_major = jnp.transpose(spectra, (3, 2, 0, 1))
    visibilities = jnp.transpose(lax.map(correlate, channel_major), (1, 0, 2, 3))
    weights_major = jnp.transpose(beam_weights, (1, 0, 2, 3))
    formed = lax.map(form_beams, (channel_major, weights_major))
    formed = formed.reshape(CHANNELS, 2, BEAMS, SPECTRA)
    arranged = jnp.transpose(formed, (1, 0, 2, 3)).reshape(2 * CHANNELS, BEAMS * SPECTRA)
    resynth = jnp.dot(matrix, arranged, precision=lax.Precision.HIGHEST, preferred_element_type=jnp.float32)
    resynth = resynth.reshape(2, CHANNELS, BEAMS, SPECTRA)
    padded_series = jnp.pad(resynth, ((0, 0), (0, 0), (0, 0), (TAPS - 1, 0)))
    series = jnp.zeros_like(resynth)
    for tap_index in range(TAPS):
        begin_at = TAPS - 1 - tap_index
        series = series + synth_taps[tap_index][None, :, None, None] * padded_series[..., begin_at:begin_at + SPECTRA]
    series = jnp.transpose(series, (0, 2, 3, 1)).reshape(2, N_BEAM, GROUP_BEAMS, SAMPLES)
    return (visibilities, series)
```

```python
import functools
import math

import jax
import jax.numpy as jnp
import numpy as np
from jax import lax
from jax.experimental import pallas as pl
from jax.experimental.pallas import tpu as pltpu
from jax.sharding import PartitionSpec as P

F32, BF16 = jnp.float32, jnp.bfloat16
MIB = 2**20


def spin_matrix(points):
    index = np.arange(points)
    angles = (index[:, None] * index[None, :] % points) * (2.0 * math.pi / points)
    cosine, sine = np.cos(angles) / math.sqrt(points), np.sin(angles) / math.sqrt(points)
    upper = np.concatenate([cosine, -sine], axis=1)
    lower = np.concatenate([sine, cosine], axis=1)
    return np.concatenate([upper, lower], axis=0).astype(np.float32)


def split(matrix):
    high = matrix.astype(jnp.bfloat16)
    low = (matrix - high.astype(np.float32)).astype(jnp.bfloat16)
    return jnp.asarray(high), jnp.asarray(low)


def dot(a, b, dims):
    return lax.dot_general(a, b, (dims, ((), ())), preferred_element_type=F32)


def front_kernel(taps, channels, v_ref, h_ref, taps_ref, high_ref, low_ref, out_ref, re_ref, im_ref, left_ref, right_ref):
    stations = v_ref.shape[1]
    spectra = v_ref.shape[2] // channels
    step = 8
    weights = [jnp.broadcast_to(taps_ref[m : m + 1, :], (stations, channels)) for m in range(taps)]

    def window(tile, t0, part, store):
        tiles = [tile(part, i - (taps - 1)) for i in range(step + taps - 1)]
        for j in range(step):
            total = weights[0] * tiles[j + taps - 1]
            for m in range(1, taps):
                total += weights[m] * tiles[j + taps - 1 - m]
            store[pl.ds((t0 + j) * stations, stations), :] = total

    for block in range(2):
        for part, store in ((0, re_ref), (1, im_ref)):

            def tile(part, i, block=block):
                t = block * step + i
                ref, at = (v_ref, t) if t >= 0 else (h_ref, t + taps - 1)
                return ref[part, :, at * channels : (at + 1) * channels].astype(F32)

            window(tile, block * step, part, store)

    @pl.loop(2, spectra // step)
    def _(block):
        for part, store in ((0, re_ref), (1, im_ref)):

            def tile(part, i):
                at = pl.multiple_of((block * step + i) * channels, channels)
                return v_ref[part, :, pl.ds(at, channels)].astype(F32)

            window(tile, block * step, part, store)

    rows = high_ref.shape[0]
    for s in range(stations):
        wide = jnp.concatenate(
            [re_ref[pl.ds(s, spectra, stride=stations), :], im_ref[pl.ds(s, spectra, stride=stations), :]], axis=1
        )
        high = wide.astype(BF16)
        low = (wide - high.astype(F32)).astype(BF16)
        nt = ((1,), (1,))
        result = dot(high_ref[...], high, nt) + dot(high_ref[...], low, nt) + dot(low_ref[...], high, nt)
        left_ref[pl.ds(s, rows, stride=stations), :] = result[:, :128]
        right_ref[pl.ds(s, rows, stride=stations), :] = result[:, 128:]

    @pl.loop(0, rows // 16)
    def _(i):
        at = pl.ds(i * 16 * stations, 16 * stations)
        out_ref[at, :128] = left_ref[at, :].astype(BF16)
        out_ref[at, 128:] = right_ref[at, :].astype(BF16)


def front(voltages, history, filter_taps):
    _, stations, samples = voltages.shape
    taps, channels = filter_taps.shape
    spectra = samples // channels
    order = np.array([ri * channels + c for c in range(channels) for ri in range(2)])
    high, low = split(spin_matrix(channels).T[order])
    vmem = pl.BlockSpec(memory_space=pltpu.VMEM)
    return pl.pallas_call(
        functools.partial(front_kernel, taps, channels),
        out_shape=jax.ShapeDtypeStruct((2 * channels * stations, spectra), BF16),
        in_specs=[vmem] * 5,
        out_specs=vmem,
        scratch_shapes=[pltpu.VMEM((spectra * stations, channels), F32)] * 2
        + [pltpu.VMEM((2 * channels * stations, 128), F32)] * 2,
        compiler_params=pltpu.CompilerParams(vmem_limit_bytes=40 * MIB),
        name="front",
    )(voltages, history, filter_taps, high, low)


def beams_kernel(quarters, w_ref, x_ref, out_ref, left_ref, right_ref):
    q = pl.program_id(1)
    groups = w_ref.shape[1] // 4
    stations = x_ref.shape[3]
    result = dot(w_ref[0, :, :stations], x_ref[0, 0, 0], ((1,), (0,)))
    result += dot(w_ref[0, :, stations:], x_ref[0, 0, 1], ((1,), (0,)))
    for i in range(4):
        rows = result[i * groups : (i + 1) * groups]
        left_ref[pl.ds(q * 4 + i, groups, stride=16), :] = rows[:, :128]
        right_ref[pl.ds(q * 4 + i, groups, stride=16), :] = rows[:, 128:]

    @pl.when(q == quarters - 1)
    def _():
        for d in range(0, groups, 8):
            at = slice(d * 16, (d + 8) * 16)
            out_ref[d : d + 8, 0, :, :128] = left_ref[at, :].astype(BF16).reshape(8, 16, 128)
            out_ref[d : d + 8, 0, :, 128:] = right_ref[at, :].astype(BF16).reshape(8, 16, 128)


def beams(weights, x):
    quarters, channels, _, stations, spectra = x.shape
    groups = weights.shape[1] // 4
    return pl.pallas_call(
        functools.partial(beams_kernel, quarters),
        grid=(channels, quarters),
        out_shape=jax.ShapeDtypeStruct((groups, channels, 16, spectra), BF16),
        in_specs=[
            pl.BlockSpec((1, 4 * groups, 2 * stations), lambda c, q: (c, 0, 0)),
            pl.BlockSpec((1, 1, 2, stations, spectra), lambda c, q: (q, c, 0, 0, 0)),
        ],
        out_specs=pl.BlockSpec((groups, 1, 16, spectra), lambda c, q: (0, c, 0, 0)),
        scratch_shapes=[pltpu.VMEM((groups * 16, 128), F32)] * 2,
        compiler_params=pltpu.CompilerParams(vmem_limit_bytes=40 * MIB),
        cost_estimate=pl.CostEstimate(flops=2 * 2**30, bytes_accessed=12 * MIB, transcendentals=0),
        name="beams",
    )(weights, x)


def pairs_kernel(scale, pick_ref, x_ref, out_ref, turned_ref, rows_ref):
    q = pl.program_id(1)
    stations = x_ref.shape[3]
    count = out_ref.shape[2]
    start = pl.multiple_of(lax.axis_index("beam") * count, count)
    for part in range(2):
        for r in range(0, stations, 256):
            turned_ref[part, r : r + 256, :] = dot(pick_ref[r : r + 256, :], x_ref[0, 0, part], ((1,), (0,))).astype(BF16)
        rows_ref[part] = turned_ref[part, pl.ds(start, count), :]
    nt = ((1,), (1,))
    for at in range(0, stations, 256):
        cols = slice(at, at + 256)
        real = dot(rows_ref[0], turned_ref[0, cols], nt) + dot(rows_ref[1], turned_ref[1, cols], nt)
        imag = dot(rows_ref[1], turned_ref[0, cols], nt) - dot(rows_ref[0], turned_ref[1, cols], nt)

        @pl.when(q == 0)
        def _():
            out_ref[0, 0, :, cols] = real * scale
            out_ref[1, 0, :, cols] = imag * scale

        @pl.when(q > 0)
        def _():
            out_ref[0, 0, :, cols] += real * scale
            out_ref[1, 0, :, cols] += imag * scale


def pairs(pick, x):
    quarters, channels, _, stations, spectra = x.shape
    return pl.pallas_call(
        functools.partial(pairs_kernel, 1.0 / (quarters * spectra)),
        grid=(channels, quarters),
        out_shape=jax.ShapeDtypeStruct((2, channels, stations // quarters, stations), F32),
        in_specs=[
            pl.BlockSpec((stations, stations), lambda c, q: (0, 0)),
            pl.BlockSpec((1, 1, 2, stations, spectra), lambda c, q: (q, c, 0, 0, 0)),
        ],
        out_specs=pl.BlockSpec((2, 1, stations // quarters, stations), lambda c, q: (0, c, 0, 0)),
        scratch_shapes=[pltpu.VMEM((2, stations, spectra), BF16), pltpu.VMEM((2, stations // quarters, spectra), BF16)],
        compiler_params=pltpu.CompilerParams(vmem_limit_bytes=40 * MIB),
        cost_estimate=pl.CostEstimate(flops=12 * 2**30, bytes_accessed=16 * MIB, transcendentals=0),
        name="pairs",
    )(pick, x)


def tail_kernel(taps, quarters, g_ref, taps_ref, high_ref, low_ref, out_ref, left_ref, right_ref, *lines):
    channels = high_ref.shape[0] // 2
    spectra = g_ref.shape[1]
    pad = 16
    left_ref[...] = g_ref[:, :128].astype(F32)
    right_ref[...] = g_ref[:, 128:].astype(F32)
    tn = ((0,), (0,))
    for line in lines:
        line[:pad, :] = jnp.zeros((pad, channels), F32)
    for j in range(2):
        for q in range(quarters):
            parts = [
                jnp.concatenate(
                    [ref[pl.ds(q * 4 + j * 2 + ri, channels, stride=16), :] for ref in (left_ref, right_ref)], axis=1
                )
                for ri in range(2)
            ]
            both = jnp.concatenate(parts, axis=0).astype(BF16)
            result = dot(both, high_ref[...], tn) + dot(both, low_ref[...], tn)
            at = slice(pad + q * spectra, pad + (q + 1) * spectra)
            lines[2 * j][at, :] = result[:, :channels]
            lines[2 * j + 1][at, :] = result[:, channels:]
    block = 64
    weights = [jnp.broadcast_to(taps_ref[m : m + 1, :], (block, channels)) for m in range(taps)]
    for j in range(2):
        for part in range(2):
            line = lines[2 * j + part]
            for t in range(0, quarters * spectra, block):
                total = weights[0] * line[pad + t : pad + t + block, :]
                for m in range(1, taps):
                    total += weights[m] * line[pad + t - m : pad + t - m + block, :]
                out_ref[part, pl.ds(2 * t + j, block, stride=2), :] = total


def tail(arrived, synth_taps, quarters):
    taps, channels = synth_taps.shape
    rows, spectra = arrived.shape
    high, low = split(spin_matrix(channels).T)
    vmem = pl.BlockSpec(memory_space=pltpu.VMEM)
    total = quarters * spectra
    return pl.pallas_call(
        functools.partial(tail_kernel, taps, quarters),
        out_shape=jax.ShapeDtypeStruct((2, 2 * total, channels), F32),
        in_specs=[vmem] * 4,
        out_specs=vmem,
        scratch_shapes=[pltpu.VMEM((rows, 128), F32)] * 2 + [pltpu.VMEM((total + 16, channels), F32)] * 4,
        compiler_params=pltpu.CompilerParams(vmem_limit_bytes=40 * MIB),
        name="tail",
    )(arrived, synth_taps, high, low)


def from_behind(block, axis, distance):
    devices = range(lax.axis_size(axis))
    route = [(i - distance, i) for i in devices if i - distance in devices]
    return lax.ppermute(block, axis, route)


def local(voltages, filter_taps, synth_taps, beam_weights, station_order):
    quarters = lax.axis_size("beam")
    owners = lax.axis_size("stn")
    taps, channels = filter_taps.shape
    rows = voltages.shape[1]
    spectra = voltages.shape[2] // channels
    stations = station_order.shape[0]
    held = channels // owners
    history = from_behind(voltages[:, :, voltages.shape[2] - (taps - 1) * channels :], "beam", 1)

    pick = (station_order[None, :] == jnp.arange(stations, dtype=jnp.int32)[:, None]).astype(BF16)
    turned = lax.dot_general(beam_weights, pick, (((3,), (0,)), ((), ())), preferred_element_type=F32).astype(BF16)
    turned = turned.reshape(2, held, owners, 2, stations).transpose(0, 1, 3, 2, 4)
    real_rows = jnp.concatenate([turned[0], -turned[1]], axis=-1)
    imag_rows = jnp.concatenate([turned[1], turned[0]], axis=-1)
    weights = jnp.stack([real_rows, imag_rows], axis=2).reshape(held, 4 * owners, 2 * stations)

    spectral = front(voltages, history, filter_taps).reshape(owners, held, 2, rows, spectra)
    mine = lax.all_to_all(spectral, "stn", split_axis=0, concat_axis=0, tiled=True)
    mine = mine.transpose(1, 2, 0, 3, 4).reshape(held, 2, stations, spectra)
    x = lax.all_gather(mine, "beam", axis=0, tiled=False)
    formed = beams(weights, x)
    arrived = lax.all_to_all(formed, "stn", split_axis=0, concat_axis=0, tiled=True)
    visibilities = pairs(pick, x)
    series = tail(arrived.reshape(-1, spectra), synth_taps, quarters)
    series = series.reshape(2, quarters * spectra, 2, channels).transpose(0, 2, 1, 3)
    return visibilities, series.reshape(2, 1, 2, quarters * spectra * channels)


def solution(mesh):
    in_specs = (P(None, "stn", "beam"), P(), P(), P(None, "stn", "beam", None), P())
    out_specs = (P(None, "stn", "beam", None), P(None, "beam", "stn", None))
    return jax.shard_map(local, mesh=mesh, in_specs=in_specs, out_specs=out_specs, check_vma=False)
```

```python
import functools
import math

import jax
import jax.numpy as jnp
import numpy as np
from jax import lax
from jax.experimental import pallas as pl
from jax.experimental.pallas import tpu as pltpu
from jax.sharding import PartitionSpec as P

F32, BF16 = jnp.float32, jnp.bfloat16
MIB = 2**20


def spin_matrix(points):
    index = np.arange(points)
    angles = (index[:, None] * index[None, :] % points) * (2.0 * math.pi / points)
    cosine, sine = np.cos(angles) / math.sqrt(points), np.sin(angles) / math.sqrt(points)
    upper = np.concatenate([cosine, -sine], axis=1)
    lower = np.concatenate([sine, cosine], axis=1)
    return np.concatenate([upper, lower], axis=0).astype(np.float32)


def split(matrix):
    high = matrix.astype(jnp.bfloat16)
    low = (matrix - high.astype(np.float32)).astype(jnp.bfloat16)
    return jnp.asarray(high), jnp.asarray(low)


def dot(a, b, dims):
    return lax.dot_general(a, b, (dims, ((), ())), preferred_element_type=F32)


def front_kernel(taps, channels, v_ref, h_ref, taps_ref, high_ref, low_ref, out_ref, re_ref, im_ref, left_ref, right_ref):
    stations = v_ref.shape[1]
    spectra = v_ref.shape[2] // channels
    step = 8
    weights = [jnp.broadcast_to(taps_ref[m : m + 1, :], (stations, channels)) for m in range(taps)]

    def window(tile, t0, part, store):
        tiles = [tile(part, i - (taps - 1)) for i in range(step + taps - 1)]
        for j in range(step):
            total = weights[0] * tiles[j + taps - 1]
            for m in range(1, taps):
                total += weights[m] * tiles[j + taps - 1 - m]
            store[pl.ds((t0 + j) * stations, stations), :] = total

    for block in range(2):
        for part, store in ((0, re_ref), (1, im_ref)):

            def tile(part, i, block=block):
                t = block * step + i
                ref, at = (v_ref, t) if t >= 0 else (h_ref, t + taps - 1)
                return ref[part, :, at * channels : (at + 1) * channels].astype(F32)

            window(tile, block * step, part, store)

    @pl.loop(2, spectra // step)
    def _(block):
        for part, store in ((0, re_ref), (1, im_ref)):

            def tile(part, i):
                at = pl.multiple_of((block * step + i) * channels, channels)
                return v_ref[part, :, pl.ds(at, channels)].astype(F32)

            window(tile, block * step, part, store)

    rows = high_ref.shape[0]
    for s in range(stations):
        wide = jnp.concatenate(
            [re_ref[pl.ds(s, spectra, stride=stations), :], im_ref[pl.ds(s, spectra, stride=stations), :]], axis=1
        )
        high = wide.astype(BF16)
        low = (wide - high.astype(F32)).astype(BF16)
        nt = ((1,), (1,))
        result = dot(high_ref[...], high, nt) + dot(high_ref[...], low, nt) + dot(low_ref[...], high, nt)
        left_ref[pl.ds(s, rows, stride=stations), :] = result[:, :128]
        right_ref[pl.ds(s, rows, stride=stations), :] = result[:, 128:]

    @pl.loop(0, rows // 16)
    def _(i):
        at = pl.ds(i * 16 * stations, 16 * stations)
        out_ref[at, :128] = left_ref[at, :].astype(BF16)
        out_ref[at, 128:] = right_ref[at, :].astype(BF16)


def front(voltages, history, filter_taps):
    _, stations, samples = voltages.shape
    taps, channels = filter_taps.shape
    spectra = samples // channels
    order = np.array([ri * channels + c for c in range(channels) for ri in range(2)])
    high, low = split(spin_matrix(channels).T[order])
    vmem = pl.BlockSpec(memory_space=pltpu.VMEM)
    return pl.pallas_call(
        functools.partial(front_kernel, taps, channels),
        out_shape=jax.ShapeDtypeStruct((2 * channels * stations, spectra), BF16),
        in_specs=[vmem] * 5,
        out_specs=vmem,
        scratch_shapes=[pltpu.VMEM((spectra * stations, channels), F32)] * 2
        + [pltpu.VMEM((2 * channels * stations, 128), F32)] * 2,
        compiler_params=pltpu.CompilerParams(vmem_limit_bytes=40 * MIB),
        name="front",
    )(voltages, history, filter_taps, high, low)

MESH = pl.DeviceIdType.MESH


def turn_kernel(sides, planes, across, s_ref, x_ref, send, arrive, forward, forwarded, share, shared):
    pairs_count = lax.axis_size("stn") // planes
    stn, beam = lax.axis_index("stn"), lax.axis_index("beam")
    p, place = stn // planes, stn % planes
    x, y = place // across, place % across
    side, core = beam // 2, beam % 2
    rows = s_ref.shape[3]
    partner, sibling = (stn, (1 - side) * 2 + core), (stn, side * 2 + 1 - core)

    def target(turns, dx, dy):
        enter = (side, 0, 1 - side, 1)[turns]
        return ((p + turns) % pairs_count) * planes + ((x + dx) % across) * across + (y + dy) % across, enter * 2 + core

    def origin(group, at):
        near = (p + 3 + 2 * at) % pairs_count
        return ((p, at), (near, 0), (near, 1), ((p + 2) % pairs_count, 1 - at))[group]

    def part(group, at, dx):
        pair, start = origin(group, at)
        first = pl.multiple_of((pair * planes + ((x + across - dx) % across) * across) * rows, across * rows)
        return x_ref.at[start * 2 + core, :, :, pl.ds(first, across * rows), :], start

    def copy(source, goal, out, into, device):
        return pltpu.make_async_remote_copy(
            src_ref=source, dst_ref=goal, send_sem=out, recv_sem=into, device_id=device, device_id_type=MESH
        )

    barrier = pltpu.get_barrier_semaphore()
    for other in (partner, sibling):
        pl.semaphore_signal(barrier, inc=1, device_id=other, device_id_type=MESH)

    @pl.loop(0, planes)
    def _(i):
        for group in range(4):
            pair, start = origin(group, side)
            other = (pair * planes + i, start * 2 + core)

            def greet(other=other):
                pl.semaphore_signal(barrier, inc=1, device_id=other, device_id_type=MESH)

            if group:
                greet()
            else:
                pl.when(i != place)(greet)

    pl.semaphore_wait(barrier, 4 * planes - 1 + 2)

    first = pl.multiple_of(stn * rows, rows)
    landing = x_ref.at[beam, :, :, pl.ds(first, rows), :]

    @pl.loop(0, planes)
    def _(i):
        dx, dy = i // across, i % across
        for turns, slot in ((2, 3), (1, 1 + side), (3, 1 + side), (0, 0)):
            owner, entry = target(turns, dx, dy)

            def go(owner=owner, entry=entry, slot=slot):
                copy(s_ref.at[owner], landing, send, arrive.at[slot, dx], (owner, entry)).start()

            if turns:
                go()
            else:
                pl.when(i != 0)(go)

                @pl.when(i == 0)
                def _():
                    pltpu.make_async_copy(s_ref.at[stn], landing, arrive.at[0, 0]).start()

    def wait(ref, sem):
        pltpu.make_async_copy(ref, ref, sem).wait()

    def entered(dx):
        for group in (3, 1, 2, 0):
            block, start = part(group, side, dx)
            wait(block, arrive.at[group, dx])
            copy(block, block, forward, forwarded.at[group, dx], partner).start()
            copy(block, block, share.at[start], shared.at[start], sibling).start()

    def passed(dx):
        for group in (3, 1, 2, 0):
            block, start = part(group, 1 - side, dx)
            wait(block, forwarded.at[group, dx])
            copy(block, block, share.at[start], shared.at[start], sibling).start()

    @pl.loop(0, across + 1)
    def _(step):
        @pl.when(step < across)
        def _():
            entered(step)

        @pl.when(step > 0)
        def _():
            passed(step - 1)

    for start in range(sides):
        wait(x_ref.at[start * 2 + 1 - core], shared.at[start])
        wait(x_ref.at[start * 2 + core], share.at[start])
    wait(x_ref.at[0], forward)
    wait(s_ref.at[pl.ds(0, 4 * planes - 1)], send)


def turn(spectral):
    owners, channels, parts, rows, spectra = spectral.shape
    quarters = lax.axis_size("beam")
    across = 4
    dma = pltpu.SemaphoreType.DMA
    return pl.pallas_call(
        functools.partial(turn_kernel, quarters // 2, across * across, across),
        out_shape=jax.ShapeDtypeStruct((quarters, channels, parts, owners * rows, spectra), BF16),
        in_specs=[pl.BlockSpec(memory_space=pl.ANY)],
        out_specs=pl.BlockSpec(memory_space=pl.ANY),
        scratch_shapes=[dma, dma((4, across)), dma, dma((4, across)), dma((2,)), dma((2,))],
        compiler_params=pltpu.CompilerParams(collective_id=0, has_side_effects=True),
        name="turn",
    )(spectral)


def beams_kernel(quarters, w_ref, x_ref, out_ref, left_ref, right_ref):
    q = pl.program_id(1)
    groups = w_ref.shape[1] // 4
    stations = x_ref.shape[3]
    result = dot(w_ref[0, :, :stations], x_ref[0, 0, 0], ((1,), (0,)))
    result += dot(w_ref[0, :, stations:], x_ref[0, 0, 1], ((1,), (0,)))
    for i in range(4):
        rows = result[i * groups : (i + 1) * groups]
        left_ref[pl.ds(q * 4 + i, groups, stride=16), :] = rows[:, :128]
        right_ref[pl.ds(q * 4 + i, groups, stride=16), :] = rows[:, 128:]

    @pl.when(q == quarters - 1)
    def _():
        for d in range(0, groups, 8):
            at = slice(d * 16, (d + 8) * 16)
            out_ref[d : d + 8, 0, :, :128] = left_ref[at, :].astype(BF16).reshape(8, 16, 128)
            out_ref[d : d + 8, 0, :, 128:] = right_ref[at, :].astype(BF16).reshape(8, 16, 128)


def beams(weights, x):
    quarters, channels, _, stations, spectra = x.shape
    groups = weights.shape[1] // 4
    return pl.pallas_call(
        functools.partial(beams_kernel, quarters),
        grid=(channels, quarters),
        out_shape=jax.ShapeDtypeStruct((groups, channels, 16, spectra), BF16),
        in_specs=[
            pl.BlockSpec((1, 4 * groups, 2 * stations), lambda c, q: (c, 0, 0)),
            pl.BlockSpec((1, 1, 2, stations, spectra), lambda c, q: (q, c, 0, 0, 0)),
        ],
        out_specs=pl.BlockSpec((groups, 1, 16, spectra), lambda c, q: (0, c, 0, 0)),
        scratch_shapes=[pltpu.VMEM((groups * 16, 128), F32)] * 2,
        compiler_params=pltpu.CompilerParams(vmem_limit_bytes=40 * MIB),
        cost_estimate=pl.CostEstimate(flops=2 * 2**30, bytes_accessed=12 * MIB, transcendentals=0),
        name="beams",
    )(weights, x)


def pairs_kernel(scale, pick_ref, x_ref, out_ref, turned_ref, rows_ref):
    q = pl.program_id(1)
    stations = x_ref.shape[3]
    count = out_ref.shape[2]
    start = pl.multiple_of(lax.axis_index("beam") * count, count)
    for part in range(2):
        for r in range(0, stations, 256):
            turned_ref[part, r : r + 256, :] = dot(pick_ref[r : r + 256, :], x_ref[0, 0, part], ((1,), (0,))).astype(BF16)
        rows_ref[part] = turned_ref[part, pl.ds(start, count), :]
    nt = ((1,), (1,))
    for at in range(0, stations, 256):
        cols = slice(at, at + 256)
        real = dot(rows_ref[0], turned_ref[0, cols], nt) + dot(rows_ref[1], turned_ref[1, cols], nt)
        imag = dot(rows_ref[1], turned_ref[0, cols], nt) - dot(rows_ref[0], turned_ref[1, cols], nt)

        @pl.when(q == 0)
        def _():
            out_ref[0, 0, :, cols] = real * scale
            out_ref[1, 0, :, cols] = imag * scale

        @pl.when(q > 0)
        def _():
            out_ref[0, 0, :, cols] += real * scale
            out_ref[1, 0, :, cols] += imag * scale


def pairs(pick, x):
    quarters, channels, _, stations, spectra = x.shape
    return pl.pallas_call(
        functools.partial(pairs_kernel, 1.0 / (quarters * spectra)),
        grid=(channels, quarters),
        out_shape=jax.ShapeDtypeStruct((2, channels, stations // quarters, stations), F32),
        in_specs=[
            pl.BlockSpec((stations, stations), lambda c, q: (0, 0)),
            pl.BlockSpec((1, 1, 2, stations, spectra), lambda c, q: (q, c, 0, 0, 0)),
        ],
        out_specs=pl.BlockSpec((2, 1, stations // quarters, stations), lambda c, q: (0, c, 0, 0)),
        scratch_shapes=[pltpu.VMEM((2, stations, spectra), BF16), pltpu.VMEM((2, stations // quarters, spectra), BF16)],
        compiler_params=pltpu.CompilerParams(vmem_limit_bytes=40 * MIB),
        cost_estimate=pl.CostEstimate(flops=12 * 2**30, bytes_accessed=16 * MIB, transcendentals=0),
        name="pairs",
    )(pick, x)


def tail_kernel(taps, quarters, g_ref, taps_ref, high_ref, low_ref, out_ref, left_ref, right_ref, *lines):
    channels = high_ref.shape[0] // 2
    spectra = g_ref.shape[1]
    pad = 16
    left_ref[...] = g_ref[:, :128].astype(F32)
    right_ref[...] = g_ref[:, 128:].astype(F32)
    tn = ((0,), (0,))
    for line in lines:
        line[:pad, :] = jnp.zeros((pad, channels), F32)
    for j in range(2):
        for q in range(quarters):
            parts = [
                jnp.concatenate(
                    [ref[pl.ds(q * 4 + j * 2 + ri, channels, stride=16), :] for ref in (left_ref, right_ref)], axis=1
                )
                for ri in range(2)
            ]
            both = jnp.concatenate(parts, axis=0).astype(BF16)
            result = dot(both, high_ref[...], tn) + dot(both, low_ref[...], tn)
            at = slice(pad + q * spectra, pad + (q + 1) * spectra)
            lines[2 * j][at, :] = result[:, :channels]
            lines[2 * j + 1][at, :] = result[:, channels:]
    block = 64
    weights = [jnp.broadcast_to(taps_ref[m : m + 1, :], (block, channels)) for m in range(taps)]
    for j in range(2):
        for part in range(2):
            line = lines[2 * j + part]
            for t in range(0, quarters * spectra, block):
                total = weights[0] * line[pad + t : pad + t + block, :]
                for m in range(1, taps):
                    total += weights[m] * line[pad + t - m : pad + t - m + block, :]
                out_ref[part, pl.ds(2 * t + j, block, stride=2), :] = total


def tail(arrived, synth_taps, quarters):
    taps, channels = synth_taps.shape
    rows, spectra = arrived.shape
    high, low = split(spin_matrix(channels).T)
    vmem = pl.BlockSpec(memory_space=pltpu.VMEM)
    total = quarters * spectra
    return pl.pallas_call(
        functools.partial(tail_kernel, taps, quarters),
        out_shape=jax.ShapeDtypeStruct((2, 2 * total, channels), F32),
        in_specs=[vmem] * 4,
        out_specs=vmem,
        scratch_shapes=[pltpu.VMEM((rows, 128), F32)] * 2 + [pltpu.VMEM((total + 16, channels), F32)] * 4,
        compiler_params=pltpu.CompilerParams(vmem_limit_bytes=40 * MIB),
        name="tail",
    )(arrived, synth_taps, high, low)


def from_behind(block, axis, distance):
    devices = range(lax.axis_size(axis))
    route = [(i - distance, i) for i in devices if i - distance in devices]
    return lax.ppermute(block, axis, route)


def local(voltages, filter_taps, synth_taps, beam_weights, station_order):
    quarters = lax.axis_size("beam")
    owners = lax.axis_size("stn")
    taps, channels = filter_taps.shape
    rows = voltages.shape[1]
    spectra = voltages.shape[2] // channels
    stations = station_order.shape[0]
    held = channels // owners
    history = from_behind(voltages[:, :, voltages.shape[2] - (taps - 1) * channels :], "beam", 1)

    pick = (station_order[None, :] == jnp.arange(stations, dtype=jnp.int32)[:, None]).astype(BF16)
    turned = lax.dot_general(beam_weights, pick, (((3,), (0,)), ((), ())), preferred_element_type=F32).astype(BF16)
    turned = turned.reshape(2, held, owners, 2, stations).transpose(0, 1, 3, 2, 4)
    real_rows = jnp.concatenate([turned[0], -turned[1]], axis=-1)
    imag_rows = jnp.concatenate([turned[1], turned[0]], axis=-1)
    weights = jnp.stack([real_rows, imag_rows], axis=2).reshape(held, 4 * owners, 2 * stations)

    spectral = front(voltages, history, filter_taps).reshape(owners, held, 2, rows, spectra)
    x = turn(spectral)
    formed = beams(weights, x)
    arrived = lax.all_to_all(formed, "stn", split_axis=0, concat_axis=0, tiled=True)
    visibilities = pairs(pick, x)
    series = tail(arrived.reshape(-1, spectra), synth_taps, quarters)
    series = series.reshape(2, quarters * spectra, 2, channels).transpose(0, 2, 1, 3)
    return visibilities, series.reshape(2, 1, 2, quarters * spectra * channels)


def solution(mesh):
    in_specs = (P(None, "stn", "beam"), P(), P(), P(None, "stn", "beam", None), P())
    out_specs = (P(None, "stn", "beam", None), P(None, "beam", "stn", None))
    return jax.shard_map(local, mesh=mesh, in_specs=in_specs, out_specs=out_specs, check_vma=False)
```

```python
import functools
import math

import jax
import jax.numpy as jnp
import numpy as np
from jax import lax
from jax.experimental import pallas as pl
from jax.experimental.pallas import tpu as pltpu
from jax.sharding import PartitionSpec as P

F32, BF16 = jnp.float32, jnp.bfloat16
MIB = 2**20


def spin_matrix(points):
    index = np.arange(points)
    angles = (index[:, None] * index[None, :] % points) * (2.0 * math.pi / points)
    cosine, sine = np.cos(angles) / math.sqrt(points), np.sin(angles) / math.sqrt(points)
    upper = np.concatenate([cosine, -sine], axis=1)
    lower = np.concatenate([sine, cosine], axis=1)
    return np.concatenate([upper, lower], axis=0).astype(np.float32)


def split(matrix):
    high = matrix.astype(jnp.bfloat16)
    low = (matrix - high.astype(np.float32)).astype(jnp.bfloat16)
    return jnp.asarray(high), jnp.asarray(low)


def dot(a, b, dims):
    return lax.dot_general(a, b, (dims, ((), ())), preferred_element_type=F32)


def front_kernel(taps, channels, v_ref, h_ref, taps_ref, high_ref, low_ref, out_ref, re_ref, im_ref, left_ref, right_ref):
    stations = v_ref.shape[1]
    spectra = v_ref.shape[2] // channels
    step = 8
    weights = [jnp.broadcast_to(taps_ref[m : m + 1, :], (stations, channels)) for m in range(taps)]

    def window(tile, t0, part, store):
        tiles = [tile(part, i - (taps - 1)) for i in range(step + taps - 1)]
        for j in range(step):
            total = weights[0] * tiles[j + taps - 1]
            for m in range(1, taps):
                total += weights[m] * tiles[j + taps - 1 - m]
            store[pl.ds((t0 + j) * stations, stations), :] = total

    for block in range(2):
        for part, store in ((0, re_ref), (1, im_ref)):

            def tile(part, i, block=block):
                t = block * step + i
                ref, at = (v_ref, t) if t >= 0 else (h_ref, t + taps - 1)
                return ref[part, :, at * channels : (at + 1) * channels].astype(F32)

            window(tile, block * step, part, store)

    @pl.loop(2, spectra // step)
    def _(block):
        for part, store in ((0, re_ref), (1, im_ref)):

            def tile(part, i):
                at = pl.multiple_of((block * step + i) * channels, channels)
                return v_ref[part, :, pl.ds(at, channels)].astype(F32)

            window(tile, block * step, part, store)

    rows = high_ref.shape[0]
    for s in range(stations):
        wide = jnp.concatenate(
            [re_ref[pl.ds(s, spectra, stride=stations), :], im_ref[pl.ds(s, spectra, stride=stations), :]], axis=1
        )
        high = wide.astype(BF16)
        low = (wide - high.astype(F32)).astype(BF16)
        nt = ((1,), (1,))
        result = dot(high_ref[...], high, nt) + dot(high_ref[...], low, nt) + dot(low_ref[...], high, nt)
        left_ref[pl.ds(s, rows, stride=stations), :] = result[:, :128]
        right_ref[pl.ds(s, rows, stride=stations), :] = result[:, 128:]

    @pl.loop(0, rows // 16)
    def _(i):
        at = pl.ds(i * 16 * stations, 16 * stations)
        out_ref[at, :128] = left_ref[at, :].astype(BF16)
        out_ref[at, 128:] = right_ref[at, :].astype(BF16)


def front(voltages, history, filter_taps):
    _, stations, samples = voltages.shape
    taps, channels = filter_taps.shape
    spectra = samples // channels
    order = np.array([ri * channels + c for c in range(channels) for ri in range(2)])
    high, low = split(spin_matrix(channels).T[order])
    vmem = pl.BlockSpec(memory_space=pltpu.VMEM)
    return pl.pallas_call(
        functools.partial(front_kernel, taps, channels),
        out_shape=jax.ShapeDtypeStruct((2 * channels * stations, spectra), BF16),
        in_specs=[vmem] * 5,
        out_specs=vmem,
        scratch_shapes=[pltpu.VMEM((spectra * stations, channels), F32)] * 2
        + [pltpu.VMEM((2 * channels * stations, 128), F32)] * 2,
        compiler_params=pltpu.CompilerParams(vmem_limit_bytes=40 * MIB),
        name="front",
    )(voltages, history, filter_taps, high, low)

MESH = pl.DeviceIdType.MESH


def remote(source, goal, out, into, device):
    return pltpu.make_async_remote_copy(
        src_ref=source, dst_ref=goal, send_sem=out, recv_sem=into, device_id=device, device_id_type=MESH
    )


def wait(ref, sem):
    pltpu.make_async_copy(ref, ref, sem).wait()


def hail(device):
    pl.semaphore_signal(pltpu.get_barrier_semaphore(), inc=1, device_id=device, device_id_type=MESH)


def turn_kernel(
    sides, planes, across, s_ref, w_ref, order_ref, x_ref, weights_ref, pick_ref,
    relay_ref, send, arrive, relayed, onward, forward, forwarded, share, shared,
):
    pairs_count = lax.axis_size("stn") // planes
    stn, beam = lax.axis_index("stn"), lax.axis_index("beam")
    p, place = stn // planes, stn % planes
    x, y = place // across, place % across
    side, core = beam // 2, beam % 2
    rows = s_ref.shape[3]
    mine, others = side * 2 + core, (1 - side) * 2 + core
    partner, sibling = (stn, others), (stn, side * 2 + 1 - core)
    near = (p + 3 + 2 * side) % pairs_count
    far = (p + 2) % pairs_count
    beyond = (p + 1 + 2 * side) % pairs_count

    def part(ref, pair, dx):
        first = pl.multiple_of((pair * planes + ((x + across - dx) % across) * across) * rows, across * rows)
        return ref.at[:, :, pl.ds(first, across * rows), :]

    def entering(at, dx):
        border = (p + 3 + 2 * at) % pairs_count
        for group, pair, start in ((1, border, at), (3, far, 1 - at), (2, border, 1 - at), (0, p, at)):
            yield group, part(x_ref.at[start * 2 + core], pair, dx), start

    hail(sibling)

    @pl.loop(0, planes)
    def _(i):
        for pair, to in ((p, others), (near, others), (far, others)):
            hail((pair * planes + i, to))

        @pl.when(i != place)
        def _():
            hail((p * planes + i, mine))

    pl.semaphore_wait(pltpu.get_barrier_semaphore(), 4 * planes)

    first = pl.multiple_of(stn * rows, rows)
    landing = x_ref.at[mine, :, :, pl.ds(first, rows), :]

    @pl.loop(0, planes)
    def _(i):
        dx, dy = i // across, i % across
        goal = ((x + dx) % across) * across + (y + dy) % across
        remote(s_ref.at[beyond * planes + goal], relay_ref.at[place], send, relayed.at[dx], (p * planes + goal, others)).start()
        remote(s_ref.at[far * planes + goal], landing, send, arrive.at[3, dx], (far * planes + goal, others)).start()
        remote(s_ref.at[near * planes + goal], landing, send, arrive.at[2, dx], (near * planes + goal, others)).start()

        @pl.when(i != 0)
        def _():
            remote(s_ref.at[p * planes + goal], landing, send, arrive.at[0, dx], (p * planes + goal, mine)).start()

        @pl.when(i == 0)
        def _():
            pltpu.make_async_copy(s_ref.at[stn], landing, arrive.at[0, 0]).start()

    stations = order_ref.shape[1]

    @pl.loop(0, stations // 64)
    def _(i):
        first = pl.multiple_of(i * 64, 64)
        station = lax.broadcasted_iota(jnp.int32, (64, stations), 0) + first
        pick_ref[pl.ds(first, 64), :] = jnp.where(order_ref[...] == station, 1.0, 0.0).astype(BF16)

    def relay(dx):
        block = relay_ref.at[pl.ds(((x + across - dx) % across) * across, across)]
        wait(block, relayed.at[dx])
        for i in range(across):
            source = (x + across - dx) % across * across + i
            first = pl.multiple_of((p * planes + source) * rows, rows)
            goal = x_ref.at[others, :, :, pl.ds(first, rows), :]
            remote(relay_ref.at[source], goal, onward, arrive.at[1, dx], (near * planes + place, others)).start()

    def entered(dx):
        for group, block, start in entering(side, dx):
            wait(block, arrive.at[group, dx])
            remote(block, block, forward, forwarded.at[group, dx], partner).start()
            remote(block, block, share.at[start], shared.at[start], sibling).start()

    def passed(dx):
        for group, block, start in entering(1 - side, dx):
            wait(block, forwarded.at[group, dx])
            remote(block, block, share.at[start], shared.at[start], sibling).start()

    @pl.loop(0, across + 2)
    def _(step):
        @pl.when(step < across)
        def _():
            relay(step)

        @pl.when((step > 0) & (step <= across))
        def _():
            entered(step - 1)

        @pl.when(step > 1)
        def _():
            passed(step - 2)

        @pl.when(step < w_ref.shape[1])
        def _():
            both = jnp.concatenate([w_ref[0, step], w_ref[1, step]], axis=0)
            half = w_ref.shape[2]
            for at in range(0, stations, 256):
                turned = dot(both, pick_ref[:, at : at + 256], ((1,), (0,)))
                weights_ref[step, :, at : at + 256] = turned.astype(BF16)
                crossed = jnp.concatenate([-turned[half:], turned[:half]], axis=0)
                weights_ref[step, :, stations + at : stations + at + 256] = crossed.astype(BF16)

    for start in range(sides):
        wait(x_ref.at[start * 2 + 1 - core], shared.at[start])
        wait(x_ref.at[start * 2 + core], share.at[start])
    wait(x_ref.at[0], forward)
    wait(relay_ref, onward)
    wait(s_ref.at[pl.ds(0, 4 * planes - 1)], send)


def turn(spectral, beam_weights, station_order):
    owners, channels, parts, rows, spectra = spectral.shape
    quarters = lax.axis_size("beam")
    across = 4
    planes = across * across
    stations, group = owners * rows, beam_weights.shape[2]
    dma = pltpu.SemaphoreType.DMA
    vmem = pl.BlockSpec(memory_space=pltpu.VMEM)
    return pl.pallas_call(
        functools.partial(turn_kernel, quarters // 2, planes, across),
        out_shape=(
            jax.ShapeDtypeStruct((quarters, channels, parts, stations, spectra), BF16),
            jax.ShapeDtypeStruct((channels, 2 * group, 2 * stations), BF16),
            jax.ShapeDtypeStruct((stations, stations), BF16),
        ),
        in_specs=[vmem] * 3,
        out_specs=(vmem,) * 3,
        scratch_shapes=[
            pltpu.VMEM((planes, channels, parts, rows, spectra), BF16),
            dma, dma((4, across)), dma((across,)), dma, dma, dma((4, across)), dma((2,)), dma((2,)),
        ],
        compiler_params=pltpu.CompilerParams(collective_id=0, has_side_effects=True, vmem_limit_bytes=28 * MIB),
        name="turn",
    )(spectral, beam_weights, station_order.reshape(1, stations))


def middle_kernel(weights_ref, x_ref, pick_ref, vis_ref, got_ref, formed_ref, turned_ref, left_ref, right_ref, send, arrive):
    stn, beam = lax.axis_index("stn"), lax.axis_index("beam")
    owners = lax.axis_size("stn")
    quarters, channels, _, stations, spectra = x_ref.shape
    group = weights_ref.shape[1] // 2

    @pl.loop(1, owners)
    def _(i):
        hail(((stn + i) % owners, beam))

    nn, nt = ((1,), (0,)), ((1,), (1,))

    @pl.loop(0, channels)
    def _(c):
        @pl.loop(0, quarters)
        def _(q):
            result = dot(weights_ref[c, :, :stations], x_ref[q, c, 0], nn)
            result += dot(weights_ref[c, :, stations:], x_ref[q, c, 1], nn)
            for part in range(2):
                rows = result[part * group : (part + 1) * group]
                left_ref[pl.ds(q * 2 + part, group, stride=8), :] = rows[:, :128]
                right_ref[pl.ds(q * 2 + part, group, stride=8), :] = rows[:, 128:]

        for d in range(0, owners, 8):
            at = slice(d * 16, (d + 8) * 16)
            formed_ref[d : d + 8, c, :, :128] = left_ref[at, :].astype(BF16).reshape(8, 16, 128)
            formed_ref[d : d + 8, c, :, 128:] = right_ref[at, :].astype(BF16).reshape(8, 16, 128)

    pl.semaphore_wait(pltpu.get_barrier_semaphore(), owners - 1)
    pltpu.make_async_copy(formed_ref.at[stn], got_ref.at[stn], arrive).start()

    @pl.loop(1, owners)
    def _(i):
        owner = (stn + i) % owners
        remote(formed_ref.at[owner], got_ref.at[stn], send, arrive, (owner, beam)).start()

    count = vis_ref.shape[2]
    start = pl.multiple_of(beam * count, count)
    scale = 1.0 / (quarters * spectra)

    @pl.loop(0, channels)
    def _(c):
        for q in range(quarters):
            at = slice(q * spectra, (q + 1) * spectra)
            for part in range(2):
                for r in range(0, stations, 256):
                    turned_ref[part, r : r + 256, at] = dot(pick_ref[r : r + 256, :], x_ref[q, c, part], nn).astype(BF16)
        real_rows = turned_ref[0, pl.ds(start, count), :]
        imag_rows = turned_ref[1, pl.ds(start, count), :]
        for at in range(0, stations, 256):
            cols = slice(at, at + 256)
            real, imag = turned_ref[0, cols, :], turned_ref[1, cols, :]
            vis_ref[0, c, :, cols] = (dot(real_rows, real, nt) + dot(imag_rows, imag, nt)) * scale
            vis_ref[1, c, :, cols] = (dot(imag_rows, real, nt) - dot(real_rows, imag, nt)) * scale

    wait(got_ref, arrive)
    wait(formed_ref.at[pl.ds(0, owners - 1)], send)


def middle(weights, x, pick):
    quarters, channels, _, stations, spectra = x.shape
    owners = lax.axis_size("stn")
    dma = pltpu.SemaphoreType.DMA
    vmem = pl.BlockSpec(memory_space=pltpu.VMEM)
    return pl.pallas_call(
        middle_kernel,
        out_shape=(
            jax.ShapeDtypeStruct((2, channels, stations // quarters, stations), F32),
            jax.ShapeDtypeStruct((owners, channels, 16, spectra), BF16),
        ),
        in_specs=[vmem] * 3,
        out_specs=(vmem,) * 2,
        scratch_shapes=[
            pltpu.VMEM((owners, channels, 16, spectra), BF16),
            pltpu.VMEM((2, stations, quarters * spectra), BF16),
            pltpu.VMEM((owners * 16, 128), F32),
            pltpu.VMEM((owners * 16, 128), F32),
            dma, dma,
        ],
        compiler_params=pltpu.CompilerParams(collective_id=1, has_side_effects=True, vmem_limit_bytes=28 * MIB),
        name="middle",
    )(weights, x, pick)


def tail_kernel(taps, quarters, g_ref, taps_ref, high_ref, low_ref, out_ref, left_ref, right_ref, *lines):
    channels = high_ref.shape[0] // 2
    spectra = g_ref.shape[1]
    pad = 16
    left_ref[...] = g_ref[:, :128].astype(F32)
    right_ref[...] = g_ref[:, 128:].astype(F32)
    tn = ((0,), (0,))
    for line in lines:
        line[:pad, :] = jnp.zeros((pad, channels), F32)
    for j in range(2):
        for q in range(quarters):
            parts = [
                jnp.concatenate(
                    [ref[pl.ds(j * 8 + q * 2 + ri, channels, stride=16), :] for ref in (left_ref, right_ref)], axis=1
                )
                for ri in range(2)
            ]
            both = jnp.concatenate(parts, axis=0).astype(BF16)
            result = dot(both, high_ref[...], tn) + dot(both, low_ref[...], tn)
            at = slice(pad + q * spectra, pad + (q + 1) * spectra)
            lines[2 * j][at, :] = result[:, :channels]
            lines[2 * j + 1][at, :] = result[:, channels:]
    block = 64
    weights = [jnp.broadcast_to(taps_ref[m : m + 1, :], (block, channels)) for m in range(taps)]
    for j in range(2):
        for part in range(2):
            line = lines[2 * j + part]
            for t in range(0, quarters * spectra, block):
                total = weights[0] * line[pad + t : pad + t + block, :]
                for m in range(1, taps):
                    total += weights[m] * line[pad + t - m : pad + t - m + block, :]
                out_ref[part, pl.ds(2 * t + j, block, stride=2), :] = total


def tail(arrived, synth_taps, quarters):
    taps, channels = synth_taps.shape
    rows, spectra = arrived.shape
    high, low = split(spin_matrix(channels).T)
    vmem = pl.BlockSpec(memory_space=pltpu.VMEM)
    total = quarters * spectra
    return pl.pallas_call(
        functools.partial(tail_kernel, taps, quarters),
        out_shape=jax.ShapeDtypeStruct((2, 2 * total, channels), F32),
        in_specs=[vmem] * 4,
        out_specs=vmem,
        scratch_shapes=[pltpu.VMEM((rows, 128), F32)] * 2 + [pltpu.VMEM((total + 16, channels), F32)] * 4,
        compiler_params=pltpu.CompilerParams(vmem_limit_bytes=40 * MIB),
        name="tail",
    )(arrived, synth_taps, high, low)


def from_behind(block, axis, distance):
    devices = range(lax.axis_size(axis))
    route = [(i - distance, i) for i in devices if i - distance in devices]
    return lax.ppermute(block, axis, route)


def local(voltages, filter_taps, synth_taps, beam_weights, station_order):
    quarters = lax.axis_size("beam")
    owners = lax.axis_size("stn")
    taps, channels = filter_taps.shape
    rows = voltages.shape[1]
    spectra = voltages.shape[2] // channels
    stations = station_order.shape[0]
    held = channels // owners
    history = from_behind(voltages[:, :, voltages.shape[2] - (taps - 1) * channels :], "beam", 1)

    spectral = front(voltages, history, filter_taps).reshape(owners, held, 2, rows, spectra)
    x, weights, pick = turn(spectral, beam_weights, station_order)
    visibilities, arrived = middle(weights, x, pick)
    series = tail(arrived.reshape(-1, spectra), synth_taps, quarters)
    series = series.reshape(2, quarters * spectra, 2, channels).transpose(0, 2, 1, 3)
    return visibilities, series.reshape(2, 1, 2, quarters * spectra * channels)


def solution(mesh):
    in_specs = (P(None, "stn", "beam"), P(), P(), P(None, "stn", "beam", None), P())
    out_specs = (P(None, "stn", "beam", None), P(None, "beam", "stn", None))
    return jax.shard_map(local, mesh=mesh, in_specs=in_specs, out_specs=out_specs, check_vma=False)
```

```python
import functools
import math

import jax
import jax.numpy as jnp
import numpy as np
from jax import lax
from jax.experimental import pallas as pl
from jax.experimental.pallas import tpu as pltpu
from jax.sharding import PartitionSpec as P

F32, BF16 = jnp.float32, jnp.bfloat16
MIB = 2**20


def spin_matrix(points):
    index = np.arange(points)
    angles = (index[:, None] * index[None, :] % points) * (2.0 * math.pi / points)
    cosine, sine = np.cos(angles) / math.sqrt(points), np.sin(angles) / math.sqrt(points)
    upper = np.concatenate([cosine, -sine], axis=1)
    lower = np.concatenate([sine, cosine], axis=1)
    return np.concatenate([upper, lower], axis=0).astype(np.float32)


def split(matrix):
    high = matrix.astype(jnp.bfloat16)
    low = (matrix - high.astype(np.float32)).astype(jnp.bfloat16)
    return jnp.asarray(high), jnp.asarray(low)


def dot(a, b, dims):
    return lax.dot_general(a, b, (dims, ((), ())), preferred_element_type=F32)


def front_kernel(taps, channels, v_ref, h_ref, taps_ref, high_ref, low_ref, out_ref, re_ref, im_ref, left_ref, right_ref):
    stations = v_ref.shape[1]
    spectra = v_ref.shape[2] // channels
    step = 8
    weights = [jnp.broadcast_to(taps_ref[m : m + 1, :], (stations, channels)) for m in range(taps)]

    def window(tile, t0, part, store):
        tiles = [tile(part, i - (taps - 1)) for i in range(step + taps - 1)]
        for j in range(step):
            total = weights[0] * tiles[j + taps - 1]
            for m in range(1, taps):
                total += weights[m] * tiles[j + taps - 1 - m]
            store[pl.ds((t0 + j) * stations, stations), :] = total

    for block in range(2):
        for part, store in ((0, re_ref), (1, im_ref)):

            def tile(part, i, block=block):
                t = block * step + i
                ref, at = (v_ref, t) if t >= 0 else (h_ref, t + taps - 1)
                return ref[part, :, at * channels : (at + 1) * channels].astype(F32)

            window(tile, block * step, part, store)

    @pl.loop(2, spectra // step)
    def _(block):
        for part, store in ((0, re_ref), (1, im_ref)):

            def tile(part, i):
                at = pl.multiple_of((block * step + i) * channels, channels)
                return v_ref[part, :, pl.ds(at, channels)].astype(F32)

            window(tile, block * step, part, store)

    rows = high_ref.shape[0]
    for s in range(stations):
        wide = jnp.concatenate(
            [re_ref[pl.ds(s, spectra, stride=stations), :], im_ref[pl.ds(s, spectra, stride=stations), :]], axis=1
        )
        high = wide.astype(BF16)
        low = (wide - high.astype(F32)).astype(BF16)
        nt = ((1,), (1,))
        result = dot(high_ref[...], high, nt) + dot(high_ref[...], low, nt) + dot(low_ref[...], high, nt)
        left_ref[pl.ds(s, rows, stride=stations), :] = result[:, :128]
        right_ref[pl.ds(s, rows, stride=stations), :] = result[:, 128:]

    @pl.loop(0, rows // 16)
    def _(i):
        at = pl.ds(i * 16 * stations, 16 * stations)
        out_ref[at, :128] = left_ref[at, :].astype(BF16)
        out_ref[at, 128:] = right_ref[at, :].astype(BF16)


def front(voltages, history, filter_taps):
    _, stations, samples = voltages.shape
    taps, channels = filter_taps.shape
    spectra = samples // channels
    order = np.array([ri * channels + c for c in range(channels) for ri in range(2)])
    high, low = split(spin_matrix(channels).T[order])
    vmem = pl.BlockSpec(memory_space=pltpu.VMEM)
    return pl.pallas_call(
        functools.partial(front_kernel, taps, channels),
        out_shape=jax.ShapeDtypeStruct((2 * channels * stations, spectra), BF16),
        in_specs=[vmem] * 5,
        out_specs=vmem,
        scratch_shapes=[pltpu.VMEM((spectra * stations, channels), F32)] * 2
        + [pltpu.VMEM((2 * channels * stations, 128), F32)] * 2,
        compiler_params=pltpu.CompilerParams(vmem_limit_bytes=40 * MIB),
        name="front",
    )(voltages, history, filter_taps, high, low)

MESH = pl.DeviceIdType.MESH


def remote(source, goal, out, into, device):
    return pltpu.make_async_remote_copy(
        src_ref=source, dst_ref=goal, send_sem=out, recv_sem=into, device_id=device, device_id_type=MESH
    )


def wait(ref, sem):
    pltpu.make_async_copy(ref, ref, sem).wait()


def hail(device):
    pl.semaphore_signal(pltpu.get_barrier_semaphore(), inc=1, device_id=device, device_id_type=MESH)


def turn_kernel(
    sides, planes, across, s_ref, w_ref, order_ref, x_ref, weights_ref, pick_ref,
    send, arrive, forward, forwarded, share, shared,
):
    pairs_count = lax.axis_size("stn") // planes
    stn, beam = lax.axis_index("stn"), lax.axis_index("beam")
    p, place = stn // planes, stn % planes
    x, y = place // across, place % across
    side, core = beam // 2, beam % 2
    rows = s_ref.shape[3]
    mine, others = side * 2 + core, (1 - side) * 2 + core
    partner, sibling = (stn, others), (stn, side * 2 + 1 - core)
    near = (p + 3 + 2 * side) % pairs_count
    far = (p + 2) % pairs_count
    beyond = (p + 1 + 2 * side) % pairs_count

    def part(ref, pair, dx):
        first = pl.multiple_of((pair * planes + ((x + across - dx) % across) * across) * rows, across * rows)
        return ref.at[:, :, pl.ds(first, across * rows), :]

    def entering(at, dx, groups):
        border = (p + 3 + 2 * at) % pairs_count
        for group in groups:
            pair, start = ((p, at), (border, at), (border, 1 - at), (far, 1 - at))[group]
            yield group, part(x_ref.at[start * 2 + core], pair, dx), start

    hail(sibling)
    hail(partner)

    @pl.loop(0, planes)
    def _(i):
        for pair, to in ((near, mine), (near, others), (far, others)):
            hail((pair * planes + i, to))

        @pl.when(i != place)
        def _():
            hail((p * planes + i, mine))

    pl.semaphore_wait(pltpu.get_barrier_semaphore(), 4 * planes + 1)

    first = pl.multiple_of(stn * rows, rows)
    landing = x_ref.at[mine, :, :, pl.ds(first, rows), :]
    pltpu.make_async_copy(s_ref.at[stn], landing, arrive.at[0, 0]).start()

    def depart(group, dx, dy):
        pair, entry = ((p, mine), (beyond, mine), (near, others), (far, others))[group]
        owner = pair * planes + ((x + dx) % across) * across + (y + dy) % across
        remote(s_ref.at[owner], landing, send, arrive.at[group, dx], (owner, entry)).start()

    @pl.loop(1, planes)
    def _(i):
        depart(0, i // across, i % across)

    @pl.loop(0, planes)
    def _(i):
        for group in (3, 1, 2):
            depart(group, i // across, i % across)

    stations = order_ref.shape[1]

    @pl.loop(0, stations // 64)
    def _(i):
        first = pl.multiple_of(i * 64, 64)
        station = lax.broadcasted_iota(jnp.int32, (64, stations), 0) + first
        pick_ref[pl.ds(first, 64), :] = jnp.where(order_ref[...] == station, 1.0, 0.0).astype(BF16)

    def entered(groups, dx):
        for group, block, start in entering(side, dx, groups):
            wait(block, arrive.at[group, dx])
            remote(block, block, forward, forwarded.at[group, dx], partner).start()
            remote(block, block, share.at[start], shared.at[start], sibling).start()

    def passed(groups, dx):
        for group, block, start in entering(1 - side, dx, groups):
            wait(block, forwarded.at[group, dx])
            remote(block, block, share.at[start], shared.at[start], sibling).start()

    def weigh(c):
        half = w_ref.shape[2]
        both = jnp.concatenate([w_ref[0, c], w_ref[1, c]], axis=0)
        for at in range(0, stations, 256):
            turned = dot(both, pick_ref[:, at : at + 256], ((1,), (0,)))
            weights_ref[c, :, at : at + 256] = turned.astype(BF16)
            crossed = jnp.concatenate([-turned[half:], turned[:half]], axis=0)
            weights_ref[c, :, stations + at : stations + at + 256] = crossed.astype(BF16)

    @pl.loop(0, across)
    def _(dx):
        entered((0,), dx)

    @pl.loop(0, across)
    def _(step):
        entered((2, 1, 3), step)

        @pl.when(step < w_ref.shape[1])
        def _():
            weigh(step)

        passed((0,), step)

        @pl.when(step > 0)
        def _():
            passed((2, 1, 3), step - 1)

    passed((2, 1, 3), across - 1)

    for start in range(sides):
        wait(x_ref.at[start * 2 + 1 - core], shared.at[start])
        wait(x_ref.at[start * 2 + core], share.at[start])
    wait(x_ref.at[0], forward)
    wait(s_ref.at[pl.ds(0, 4 * planes - 1)], send)


def turn(spectral, beam_weights, station_order):
    owners, channels, parts, rows, spectra = spectral.shape
    quarters = lax.axis_size("beam")
    across = 4
    planes = across * across
    stations, group = owners * rows, beam_weights.shape[2]
    dma = pltpu.SemaphoreType.DMA
    vmem = pl.BlockSpec(memory_space=pltpu.VMEM)
    return pl.pallas_call(
        functools.partial(turn_kernel, quarters // 2, planes, across),
        out_shape=(
            jax.ShapeDtypeStruct((quarters, channels, parts, stations, spectra), BF16),
            jax.ShapeDtypeStruct((channels, 2 * group, 2 * stations), BF16),
            jax.ShapeDtypeStruct((stations, stations), BF16),
        ),
        in_specs=[vmem] * 3,
        out_specs=(vmem,) * 3,
        scratch_shapes=[
            dma, dma((4, across)), dma, dma((4, across)), dma((2,)), dma((2,)),
        ],
        compiler_params=pltpu.CompilerParams(collective_id=0, has_side_effects=True, vmem_limit_bytes=28 * MIB),
        name="turn",
    )(spectral, beam_weights, station_order.reshape(1, stations))


def middle_kernel(weights_ref, x_ref, pick_ref, vis_ref, got_ref, formed_ref, turned_ref, left_ref, right_ref, send, arrive):
    stn, beam = lax.axis_index("stn"), lax.axis_index("beam")
    owners = lax.axis_size("stn")
    quarters, channels, _, stations, spectra = x_ref.shape
    group = weights_ref.shape[1] // 2

    @pl.loop(1, owners)
    def _(i):
        hail(((stn + i) % owners, beam))

    nn, nt = ((1,), (0,)), ((1,), (1,))

    @pl.loop(0, channels)
    def _(c):
        @pl.loop(0, quarters)
        def _(q):
            result = dot(weights_ref[c, :, :stations], x_ref[q, c, 0], nn)
            result += dot(weights_ref[c, :, stations:], x_ref[q, c, 1], nn)
            for part in range(2):
                rows = result[part * group : (part + 1) * group]
                left_ref[pl.ds(q * 2 + part, group, stride=8), :] = rows[:, :128]
                right_ref[pl.ds(q * 2 + part, group, stride=8), :] = rows[:, 128:]

        for d in range(0, owners, 8):
            at = slice(d * 16, (d + 8) * 16)
            formed_ref[d : d + 8, c, :, :128] = left_ref[at, :].astype(BF16).reshape(8, 16, 128)
            formed_ref[d : d + 8, c, :, 128:] = right_ref[at, :].astype(BF16).reshape(8, 16, 128)

    pl.semaphore_wait(pltpu.get_barrier_semaphore(), owners - 1)
    pltpu.make_async_copy(formed_ref.at[stn], got_ref.at[stn], arrive).start()

    @pl.loop(1, owners)
    def _(i):
        owner = (stn + i) % owners
        remote(formed_ref.at[owner], got_ref.at[stn], send, arrive, (owner, beam)).start()

    count = vis_ref.shape[2]
    start = pl.multiple_of(beam * count, count)
    scale = 1.0 / (quarters * spectra)

    @pl.loop(0, channels)
    def _(c):
        for q in range(quarters):
            at = slice(q * spectra, (q + 1) * spectra)
            for part in range(2):
                for r in range(0, stations, 256):
                    turned_ref[part, r : r + 256, at] = dot(pick_ref[r : r + 256, :], x_ref[q, c, part], nn).astype(BF16)
        real_rows = turned_ref[0, pl.ds(start, count), :]
        imag_rows = turned_ref[1, pl.ds(start, count), :]
        for at in range(0, stations, 256):
            cols = slice(at, at + 256)
            real, imag = turned_ref[0, cols, :], turned_ref[1, cols, :]
            vis_ref[0, c, :, cols] = (dot(real_rows, real, nt) + dot(imag_rows, imag, nt)) * scale
            vis_ref[1, c, :, cols] = (dot(imag_rows, real, nt) - dot(real_rows, imag, nt)) * scale

    wait(got_ref, arrive)
    wait(formed_ref.at[pl.ds(0, owners - 1)], send)


def middle(weights, x, pick):
    quarters, channels, _, stations, spectra = x.shape
    owners = lax.axis_size("stn")
    dma = pltpu.SemaphoreType.DMA
    vmem = pl.BlockSpec(memory_space=pltpu.VMEM)
    return pl.pallas_call(
        middle_kernel,
        out_shape=(
            jax.ShapeDtypeStruct((2, channels, stations // quarters, stations), F32),
            jax.ShapeDtypeStruct((owners, channels, 16, spectra), BF16),
        ),
        in_specs=[vmem] * 3,
        out_specs=(vmem,) * 2,
        scratch_shapes=[
            pltpu.VMEM((owners, channels, 16, spectra), BF16),
            pltpu.VMEM((2, stations, quarters * spectra), BF16),
            pltpu.VMEM((owners * 16, 128), F32),
            pltpu.VMEM((owners * 16, 128), F32),
            dma, dma,
        ],
        compiler_params=pltpu.CompilerParams(collective_id=1, has_side_effects=True, vmem_limit_bytes=28 * MIB),
        name="middle",
    )(weights, x, pick)


def tail_kernel(
    taps, quarters, g_ref, vis_ref, taps_ref, high_ref, low_ref, out_ref, kept_ref, saved, left_ref, right_ref, *lines
):
    save = pltpu.make_async_copy(vis_ref, kept_ref, saved)
    save.start()
    channels = high_ref.shape[0] // 2
    spectra = g_ref.shape[1]
    pad = 16
    left_ref[...] = g_ref[:, :128].astype(F32)
    right_ref[...] = g_ref[:, 128:].astype(F32)
    tn = ((0,), (0,))
    for line in lines:
        line[:pad, :] = jnp.zeros((pad, channels), F32)
    for j in range(2):
        for q in range(quarters):
            parts = [
                jnp.concatenate(
                    [ref[pl.ds(j * 8 + q * 2 + ri, channels, stride=16), :] for ref in (left_ref, right_ref)], axis=1
                )
                for ri in range(2)
            ]
            both = jnp.concatenate(parts, axis=0).astype(BF16)
            result = dot(both, high_ref[...], tn) + dot(both, low_ref[...], tn)
            at = slice(pad + q * spectra, pad + (q + 1) * spectra)
            lines[2 * j][at, :] = result[:, :channels]
            lines[2 * j + 1][at, :] = result[:, channels:]
    block = 64
    weights = [jnp.broadcast_to(taps_ref[m : m + 1, :], (block, channels)) for m in range(taps)]
    for j in range(2):
        for part in range(2):
            line = lines[2 * j + part]
            for t in range(0, quarters * spectra, block):
                total = weights[0] * line[pad + t : pad + t + block, :]
                for m in range(1, taps):
                    total += weights[m] * line[pad + t - m : pad + t - m + block, :]
                out_ref[part, pl.ds(2 * t + j, block, stride=2), :] = total
    save.wait()


def tail(arrived, visibilities, synth_taps, quarters):
    taps, channels = synth_taps.shape
    rows, spectra = arrived.shape
    high, low = split(spin_matrix(channels).T)
    vmem = pl.BlockSpec(memory_space=pltpu.VMEM)
    total = quarters * spectra
    return pl.pallas_call(
        functools.partial(tail_kernel, taps, quarters),
        out_shape=(
            jax.ShapeDtypeStruct((2, 2 * total, channels), F32),
            jax.ShapeDtypeStruct(visibilities.shape, F32),
        ),
        in_specs=[vmem] * 5,
        out_specs=(vmem, pl.BlockSpec(memory_space=pl.ANY)),
        scratch_shapes=[pltpu.SemaphoreType.DMA]
        + [pltpu.VMEM((rows, 128), F32)] * 2 + [pltpu.VMEM((total + 16, channels), F32)] * 4,
        compiler_params=pltpu.CompilerParams(vmem_limit_bytes=40 * MIB),
        name="tail",
    )(arrived, visibilities, synth_taps, high, low)


def from_behind(block, axis, distance):
    devices = range(lax.axis_size(axis))
    route = [(i - distance, i) for i in devices if i - distance in devices]
    return lax.ppermute(block, axis, route)


def local(voltages, filter_taps, synth_taps, beam_weights, station_order):
    quarters = lax.axis_size("beam")
    owners = lax.axis_size("stn")
    taps, channels = filter_taps.shape
    rows = voltages.shape[1]
    spectra = voltages.shape[2] // channels
    stations = station_order.shape[0]
    held = channels // owners
    history = from_behind(voltages[:, :, voltages.shape[2] - (taps - 1) * channels :], "beam", 1)

    spectral = front(voltages, history, filter_taps).reshape(owners, held, 2, rows, spectra)
    x, weights, pick = turn(spectral, beam_weights, station_order)
    visibilities, arrived = middle(weights, x, pick)
    series, visibilities = tail(arrived.reshape(-1, spectra), visibilities, synth_taps, quarters)
    series = series.reshape(2, quarters * spectra, 2, channels).transpose(0, 2, 1, 3)
    return visibilities, series.reshape(2, 1, 2, quarters * spectra * channels)


def solution(mesh):
    in_specs = (P(None, "stn", "beam"), P(), P(), P(None, "stn", "beam", None), P())
    out_specs = (P(None, "stn", "beam", None), P(None, "beam", "stn", None))
    return jax.shard_map(local, mesh=mesh, in_specs=in_specs, out_specs=out_specs, check_vma=False)
```

```python
import functools
import math

import jax
import jax.numpy as jnp
import numpy as np
from jax import lax
from jax.experimental import pallas as pl
from jax.experimental.pallas import tpu as pltpu
from jax.sharding import PartitionSpec as P

F32, BF16 = jnp.float32, jnp.bfloat16
MIB = 2**20


def spin_matrix(points):
    index = np.arange(points)
    angles = (index[:, None] * index[None, :] % points) * (2.0 * math.pi / points)
    cosine, sine = np.cos(angles) / math.sqrt(points), np.sin(angles) / math.sqrt(points)
    upper = np.concatenate([cosine, -sine], axis=1)
    lower = np.concatenate([sine, cosine], axis=1)
    return np.concatenate([upper, lower], axis=0).astype(np.float32)


def split(matrix):
    high = matrix.astype(jnp.bfloat16)
    low = (matrix - high.astype(np.float32)).astype(jnp.bfloat16)
    return jnp.asarray(high), jnp.asarray(low)


def dot(a, b, dims):
    return lax.dot_general(a, b, (dims, ((), ())), preferred_element_type=F32)


MESH = pl.DeviceIdType.MESH


def remote(source, goal, out, into, device):
    return pltpu.make_async_remote_copy(
        src_ref=source, dst_ref=goal, send_sem=out, recv_sem=into, device_id=device, device_id_type=MESH
    )


def wait(ref, sem):
    pltpu.make_async_copy(ref, ref, sem).wait()


def hail(device):
    pl.semaphore_signal(pltpu.get_barrier_semaphore(), inc=1, device_id=device, device_id_type=MESH)


def fir(taps, tile, weights, t0, store):
    step, rows = 8, weights[0].shape[0]
    tiles = [tile(i - (taps - 1)) for i in range(step + taps - 1)]
    for j in range(step):
        total = weights[0] * tiles[j + taps - 1]
        for m in range(1, taps):
            total += weights[m] * tiles[j + taps - 1 - m]
        store[pl.ds((t0 + j) * rows, rows), :] = total


def main_kernel(
    sides, planes, across, v_hbm, w_hbm, taps_hbm, high_hbm, low_hbm, order_ref, vis_hbm, got_ref,
    v_ref, w_ref, taps_ref, high_ref, low_ref, rim_ref, re_ref, im_ref, left_ref, right_ref, s_ref, x_ref, weights_ref,
    pick_ref, formed_ref, turned_ref, vis_ref, loads, saves, rim_send, rim_arrive, send, arrive, forward, forwarded, share, shared,
    beam_send, beam_arrive,
):
    owners = lax.axis_size("stn")
    pairs_count = owners // planes
    stn, beam = lax.axis_index("stn"), lax.axis_index("beam")
    p, place = stn // planes, stn % planes
    x, y = place // across, place % across
    side, core = beam // 2, beam % 2
    quarters, channels, _, stations, spectra = x_ref.shape
    rows = s_ref.shape[3]
    taps, points = taps_ref.shape
    mine, others = side * 2 + core, (1 - side) * 2 + core
    partner, sibling = (stn, others), (stn, side * 2 + 1 - core)
    later, sooner = (stn, (beam + 1) % quarters), (stn, (beam + quarters - 1) % quarters)
    near = (p + 3 + 2 * side) % pairs_count
    far = (p + 2) % pairs_count
    beyond = (p + 1 + 2 * side) % pairs_count
    nn, nt = ((1,), (0,)), ((1,), (1,))

    pieces = ((v_hbm, v_ref), (taps_hbm, taps_ref), (high_hbm, high_ref), (low_hbm, low_ref), (w_hbm, w_ref))
    fetches = [pltpu.make_async_copy(a, b, loads.at[i]) for i, (a, b) in enumerate(pieces)]
    for fetch in fetches:
        fetch.start()

    hail(sibling)
    hail(partner)
    hail(sooner)

    @pl.loop(1, owners)
    def _(i):
        hail(((stn + i) % owners, beam))

    @pl.loop(0, planes)
    def _(i):
        hail((near * planes + i, others))
        hail((far * planes + i, others))

    fetches[0].wait()
    fetches[1].wait()
    filters = [jnp.broadcast_to(taps_ref[m : m + 1, :], (rows, points)) for m in range(taps)]
    stores = (re_ref, im_ref)

    @pl.loop(2, spectra // 8)
    def _(block):
        for part in range(2):

            def tile(i, part=part):
                return v_ref[part, :, pl.ds(pl.multiple_of((block * 8 + i) * points, points), points)].astype(F32)

            fir(taps, tile, filters, block * 8, stores[part])

    pl.semaphore_wait(pltpu.get_barrier_semaphore(), owners - 1 + 2 * planes + 3)
    rim = (taps - 1) * points
    remote(v_ref.at[:, :, pl.ds((spectra - taps + 1) * points, rim)], rim_ref, rim_send, rim_arrive, later).start()

    @pl.loop(0, stations // 64)
    def _(i):
        first = pl.multiple_of(i * 64, 64)
        station = lax.broadcasted_iota(jnp.int32, (64, stations), 0) + first
        pick_ref[pl.ds(first, 64), :] = jnp.where(order_ref[...] == station, 1.0, 0.0).astype(BF16)

    wait(rim_ref, rim_arrive)
    for block in range(2):
        for part in range(2):

            def tile(i, block=block, part=part):
                t = block * 8 + i
                if t >= 0:
                    return v_ref[part, :, t * points : (t + 1) * points].astype(F32)
                t += taps - 1
                before = rim_ref[part, :, t * points : (t + 1) * points].astype(F32)
                return jnp.where(beam > 0, before, jnp.zeros_like(before))

            fir(taps, tile, filters, block * 8, stores[part])

    fetches[2].wait()
    fetches[3].wait()
    lines = 2 * points
    for i in range(rows):
        at = pl.ds(i, spectra, stride=rows)
        wide = jnp.concatenate([re_ref[at, :], im_ref[at, :]], axis=1)
        high = wide.astype(BF16)
        low = (wide - high.astype(F32)).astype(BF16)
        result = dot(high_ref[...], high, nt) + dot(high_ref[...], low, nt) + dot(low_ref[...], high, nt)
        left_ref[pl.ds(i, lines, stride=rows), :] = result[:, :128]
        right_ref[pl.ds(i, lines, stride=rows), :] = result[:, 128:]

    @pl.loop(0, owners // 4)
    def _(i):
        count = channels * 2 * rows
        for j in range(4):
            at = pl.ds(pl.multiple_of((i * 4 + j) * count, count), count)
            s_ref[i * 4 + j, :, :, :, :128] = left_ref[at, :].astype(BF16).reshape(channels, 2, rows, 128)
            s_ref[i * 4 + j, :, :, :, 128:] = right_ref[at, :].astype(BF16).reshape(channels, 2, rows, 128)

    def entering(at, dx, groups):
        border = (p + 3 + 2 * at) % pairs_count
        for group in groups:
            pair, start = ((p, at), (border, at), (border, 1 - at), (far, 1 - at))[group]
            first = pl.multiple_of((pair * planes + ((x + across - dx) % across) * across) * rows, across * rows)
            yield group, x_ref.at[start * 2 + core, :, :, pl.ds(first, across * rows), :], start

    landing = x_ref.at[mine, :, :, pl.ds(pl.multiple_of(stn * rows, rows), rows), :]
    pltpu.make_async_copy(s_ref.at[stn], landing, arrive.at[0, 0]).start()

    def depart(group, dx, dy):
        pair, entry = ((p, mine), (beyond, mine), (near, others), (far, others))[group]
        owner = pair * planes + ((x + dx) % across) * across + (y + dy) % across
        remote(s_ref.at[owner], landing, send, arrive.at[group, dx], (owner, entry)).start()

    @pl.loop(1, planes)
    def _(i):
        depart(0, i // across, i % across)

    @pl.loop(0, planes)
    def _(i):
        for group in (3, 1, 2):
            depart(group, i // across, i % across)

    def entered(groups, dx):
        for group, block, start in entering(side, dx, groups):
            wait(block, arrive.at[group, dx])
            remote(block, block, forward, forwarded.at[group, dx], partner).start()
            remote(block, block, share.at[start], shared.at[start], sibling).start()

    def passed(groups, dx):
        for group, block, start in entering(1 - side, dx, groups):
            wait(block, forwarded.at[group, dx])
            remote(block, block, share.at[start], shared.at[start], sibling).start()

    half = w_ref.shape[2]

    def weigh(c):
        both = jnp.concatenate([w_ref[0, c], w_ref[1, c]], axis=0)
        for at in range(0, stations, 256):
            turned = dot(both, pick_ref[:, at : at + 256], nn)
            weights_ref[c, :, at : at + 256] = turned.astype(BF16)
            crossed = jnp.concatenate([-turned[half:], turned[:half]], axis=0)
            weights_ref[c, :, stations + at : stations + at + 256] = crossed.astype(BF16)

    @pl.loop(0, across)
    def _(dx):
        entered((0,), dx)

    fetches[4].wait()

    @pl.loop(0, across)
    def _(step):
        entered((2, 1, 3), step)

        @pl.when(step < channels)
        def _():
            weigh(step)

        passed((0,), step)

        @pl.when(step > 0)
        def _():
            passed((2, 1, 3), step - 1)

    passed((2, 1, 3), across - 1)
    for start in range(sides):
        wait(x_ref.at[start * 2 + 1 - core], shared.at[start])

    @pl.loop(0, channels)
    def _(c):
        @pl.loop(0, quarters)
        def _(q):
            result = dot(weights_ref[c, :, :stations], x_ref[q, c, 0], nn)
            result += dot(weights_ref[c, :, stations:], x_ref[q, c, 1], nn)
            for part in range(2):
                beams = result[part * half : (part + 1) * half]
                left_ref[pl.ds(q * 2 + part, half, stride=8), :] = beams[:, :128]
                right_ref[pl.ds(q * 2 + part, half, stride=8), :] = beams[:, 128:]

        for d in range(0, owners, 8):
            at = slice(d * 16, (d + 8) * 16)
            formed_ref[c, d : d + 8, :, :128] = left_ref[at, :].astype(BF16).reshape(8, 16, 128)
            formed_ref[c, d : d + 8, :, 128:] = right_ref[at, :].astype(BF16).reshape(8, 16, 128)

        pltpu.make_async_copy(formed_ref.at[c, stn], got_ref.at[c, stn], beam_arrive.at[c]).start()

        @pl.loop(1, owners)
        def _(i):
            owner = (stn + i) % owners
            remote(formed_ref.at[c, owner], got_ref.at[c, stn], beam_send.at[c], beam_arrive.at[c], (owner, beam)).start()

    count = vis_ref.shape[2]
    start = pl.multiple_of(beam * count, count)
    scale = 1.0 / (quarters * spectra)

    @pl.loop(0, channels)
    def _(c):
        for q in range(quarters):
            at = slice(q * spectra, (q + 1) * spectra)
            for part in range(2):
                for r in range(0, stations, 256):
                    turned_ref[part, r : r + 256, at] = dot(pick_ref[r : r + 256, :], x_ref[q, c, part], nn).astype(BF16)
        real_rows = turned_ref[0, pl.ds(start, count), :]
        imag_rows = turned_ref[1, pl.ds(start, count), :]
        for at in range(0, stations, 256):
            cols = slice(at, at + 256)
            real, imag = turned_ref[0, cols, :], turned_ref[1, cols, :]
            vis_ref[0, c, :, cols] = (dot(real_rows, real, nt) + dot(imag_rows, imag, nt)) * scale
            vis_ref[1, c, :, cols] = (dot(imag_rows, real, nt) - dot(real_rows, imag, nt)) * scale
        pltpu.make_async_copy(vis_ref.at[:, c], vis_hbm.at[:, c], saves.at[c]).start()

    for start in range(sides):
        wait(x_ref.at[start * 2 + core], share.at[start])
    wait(x_ref.at[0], forward)
    wait(s_ref.at[pl.ds(0, owners - 1)], send)
    wait(rim_ref, rim_send)
    for c in range(channels):
        wait(vis_ref.at[:, c], saves.at[c])
        wait(got_ref.at[c], beam_arrive.at[c])
        wait(formed_ref.at[c, pl.ds(0, owners - 1)], beam_send.at[c])


def main(voltages, beam_weights, filter_taps, station_order):
    quarters, owners = lax.axis_size("beam"), lax.axis_size("stn")
    taps, points = filter_taps.shape
    rows, spectra = voltages.shape[1], voltages.shape[2] // points
    channels, half, stations = beam_weights.shape[1:]
    across = 4
    order = np.array([ri * points + c for c in range(points) for ri in range(2)])
    high, low = split(spin_matrix(points).T[order])
    dma = pltpu.SemaphoreType.DMA
    vmem, anywhere = pl.BlockSpec(memory_space=pltpu.VMEM), pl.BlockSpec(memory_space=pl.ANY)
    return pl.pallas_call(
        functools.partial(main_kernel, quarters // 2, across * across, across),
        out_shape=(
            jax.ShapeDtypeStruct((2, channels, stations // quarters, stations), F32),
            jax.ShapeDtypeStruct((channels, owners, 16, spectra), BF16),
        ),
        in_specs=[anywhere] * 5 + [vmem],
        out_specs=(anywhere, anywhere),
        scratch_shapes=[
            pltpu.VMEM(voltages.shape, BF16),
            pltpu.VMEM(beam_weights.shape, BF16),
            pltpu.VMEM(filter_taps.shape, F32),
            pltpu.VMEM(high.shape, BF16),
            pltpu.VMEM(low.shape, BF16),
            pltpu.VMEM((2, rows, (taps - 1) * points), BF16),
            pltpu.VMEM((spectra * rows, points), F32),
            pltpu.VMEM((spectra * rows, points), F32),
            pltpu.VMEM((2 * points * rows, 128), F32),
            pltpu.VMEM((2 * points * rows, 128), F32),
            pltpu.VMEM((owners, channels, 2, rows, spectra), BF16),
            pltpu.VMEM((quarters, channels, 2, stations, spectra), BF16),
            pltpu.VMEM((channels, 2 * half, 2 * stations), BF16),
            pltpu.VMEM((stations, stations), BF16),
            pltpu.VMEM((channels, owners, 16, spectra), BF16),
            pltpu.VMEM((2, stations, quarters * spectra), BF16),
            pltpu.VMEM((2, channels, stations // quarters, stations), F32),
            dma((5,)), dma((channels,)), dma, dma, dma, dma((4, across)), dma, dma((4, across)), dma((2,)), dma((2,)),
            dma((channels,)), dma((channels,)),
        ],
        compiler_params=pltpu.CompilerParams(collective_id=0, has_side_effects=True, vmem_limit_bytes=54 * MIB),
        name="main",
    )(voltages, beam_weights, filter_taps, high, low, station_order.reshape(1, stations))


def tail_kernel(
    taps, quarters, g_ref, vis_ref, taps_ref, high_ref, low_ref, out_ref, kept_ref, saved, left_ref, right_ref, *lines
):
    save = pltpu.make_async_copy(vis_ref, kept_ref, saved)
    save.start()
    channels = high_ref.shape[0] // 2
    spectra = g_ref.shape[1]
    pad = 16
    left_ref[...] = g_ref[:, :128].astype(F32)
    right_ref[...] = g_ref[:, 128:].astype(F32)
    tn = ((0,), (0,))
    for line in lines:
        line[:pad, :] = jnp.zeros((pad, channels), F32)
    for j in range(2):
        for q in range(quarters):
            parts = [
                jnp.concatenate(
                    [ref[pl.ds(j * 8 + q * 2 + ri, channels, stride=16), :] for ref in (left_ref, right_ref)], axis=1
                )
                for ri in range(2)
            ]
            both = jnp.concatenate(parts, axis=0).astype(BF16)
            result = dot(both, high_ref[...], tn) + dot(both, low_ref[...], tn)
            at = slice(pad + q * spectra, pad + (q + 1) * spectra)
            lines[2 * j][at, :] = result[:, :channels]
            lines[2 * j + 1][at, :] = result[:, channels:]
    block = 64
    weights = [jnp.broadcast_to(taps_ref[m : m + 1, :], (block, channels)) for m in range(taps)]
    for j in range(2):
        for part in range(2):
            line = lines[2 * j + part]
            for t in range(0, quarters * spectra, block):
                total = weights[0] * line[pad + t : pad + t + block, :]
                for m in range(1, taps):
                    total += weights[m] * line[pad + t - m : pad + t - m + block, :]
                out_ref[part, pl.ds(2 * t + j, block, stride=2), :] = total
    save.wait()


def tail(arrived, visibilities, synth_taps, quarters, owners):
    taps, channels = synth_taps.shape
    rows, spectra = arrived.shape
    order = np.arange(2 * channels).reshape(2, owners, channels // owners).transpose(0, 2, 1).reshape(-1)
    high, low = split(spin_matrix(channels).T[order])
    vmem = pl.BlockSpec(memory_space=pltpu.VMEM)
    total = quarters * spectra
    return pl.pallas_call(
        functools.partial(tail_kernel, taps, quarters),
        out_shape=(
            jax.ShapeDtypeStruct((2, 2 * total, channels), F32),
            jax.ShapeDtypeStruct(visibilities.shape, F32),
        ),
        in_specs=[vmem, pl.BlockSpec(memory_space=pl.ANY), vmem, vmem, vmem],
        out_specs=(vmem, pl.BlockSpec(memory_space=pl.ANY)),
        scratch_shapes=[pltpu.SemaphoreType.DMA]
        + [pltpu.VMEM((rows, 128), F32)] * 2 + [pltpu.VMEM((total + 16, channels), F32)] * 4,
        compiler_params=pltpu.CompilerParams(vmem_limit_bytes=57 * MIB),
        name="tail",
    )(arrived, visibilities, synth_taps, high, low)


def local(voltages, filter_taps, synth_taps, beam_weights, station_order):
    quarters, owners = lax.axis_size("beam"), lax.axis_size("stn")
    channels = filter_taps.shape[1]
    spectra = voltages.shape[2] // channels
    visibilities, arrived = main(voltages, beam_weights, filter_taps, station_order)
    series, visibilities = tail(arrived.reshape(-1, spectra), visibilities, synth_taps, quarters, owners)
    series = series.reshape(2, quarters * spectra, 2, channels).transpose(0, 2, 1, 3)
    return visibilities, series.reshape(2, 1, 2, quarters * spectra * channels)


def solution(mesh):
    in_specs = (P(None, "stn", "beam"), P(), P(), P(None, "stn", "beam", None), P())
    out_specs = (P(None, "stn", "beam", None), P(None, "beam", "stn", None))
    return jax.shard_map(local, mesh=mesh, in_specs=in_specs, out_specs=out_specs, check_vma=False)
```

```python
import functools
import math

import jax
import jax.numpy as jnp
import numpy as np
from jax import lax
from jax.experimental import pallas as pl
from jax.experimental.pallas import tpu as pltpu
from jax.sharding import PartitionSpec as P

F32, BF16 = jnp.float32, jnp.bfloat16
MIB = 2**20


def spin_matrix(points):
    index = np.arange(points)
    angles = (index[:, None] * index[None, :] % points) * (2.0 * math.pi / points)
    cosine, sine = np.cos(angles) / math.sqrt(points), np.sin(angles) / math.sqrt(points)
    upper = np.concatenate([cosine, -sine], axis=1)
    lower = np.concatenate([sine, cosine], axis=1)
    return np.concatenate([upper, lower], axis=0).astype(np.float32)


def split(matrix):
    high = matrix.astype(jnp.bfloat16)
    low = (matrix - high.astype(np.float32)).astype(jnp.bfloat16)
    return jnp.asarray(high), jnp.asarray(low)


def dot(a, b, dims):
    return lax.dot_general(a, b, (dims, ((), ())), preferred_element_type=F32)


MESH = pl.DeviceIdType.MESH


def remote(source, goal, out, into, device):
    return pltpu.make_async_remote_copy(
        src_ref=source, dst_ref=goal, send_sem=out, recv_sem=into, device_id=device, device_id_type=MESH
    )


def wait(ref, sem):
    pltpu.make_async_copy(ref, ref, sem).wait()


def hail(device):
    pl.semaphore_signal(pltpu.get_barrier_semaphore(), inc=1, device_id=device, device_id_type=MESH)


def fir(taps, tile, weights, t0, store):
    step, rows = 8, weights[0].shape[0]
    tiles = [tile(i - (taps - 1)) for i in range(step + taps - 1)]
    for j in range(step):
        total = weights[0] * tiles[j + taps - 1]
        for m in range(1, taps):
            total += weights[m] * tiles[j + taps - 1 - m]
        store[pl.ds((t0 + j) * rows, rows), :] = total


def main_kernel(
    sides, planes, across, v_hbm, w_hbm, taps_hbm, high_hbm, low_hbm, order_ref, vis_hbm, got_ref,
    v_ref, w_ref, taps_ref, high_ref, low_ref, rim_ref, re_ref, im_ref, left_ref, right_ref, s_ref, x_ref, weights_ref,
    pick_ref, formed_ref, turned_ref, vis_ref, loads, saves, rim_send, rim_arrive, send, arrive, forward, forwarded, share, shared,
    beam_send, beam_arrive,
):
    owners = lax.axis_size("stn")
    pairs_count = owners // planes
    stn, beam = lax.axis_index("stn"), lax.axis_index("beam")
    p, place = stn // planes, stn % planes
    x, y = place // across, place % across
    side, core = beam // 2, beam % 2
    quarters, channels, _, stations, spectra = x_ref.shape
    rows = s_ref.shape[3]
    taps, points = taps_ref.shape
    mine, others = side * 2 + core, (1 - side) * 2 + core
    partner, sibling = (stn, others), (stn, side * 2 + 1 - core)
    later, sooner = (stn, (beam + 1) % quarters), (stn, (beam + quarters - 1) % quarters)
    near = (p + 3 + 2 * side) % pairs_count
    far = (p + 2) % pairs_count
    beyond = (p + 1 + 2 * side) % pairs_count
    nn, nt = ((1,), (0,)), ((1,), (1,))

    pieces = ((v_hbm, v_ref), (taps_hbm, taps_ref), (high_hbm, high_ref), (low_hbm, low_ref), (w_hbm, w_ref))
    fetches = [pltpu.make_async_copy(a, b, loads.at[i]) for i, (a, b) in enumerate(pieces)]
    for fetch in fetches:
        fetch.start()

    hail(sibling)
    hail(partner)
    hail(sooner)

    @pl.loop(1, owners)
    def _(i):
        hail(((stn + i) % owners, beam))

    @pl.loop(0, planes)
    def _(i):
        hail((near * planes + i, others))
        hail((far * planes + i, others))

    fetches[0].wait()
    fetches[1].wait()
    filters = [jnp.broadcast_to(taps_ref[m : m + 1, :], (rows, points)) for m in range(taps)]
    stores = (re_ref, im_ref)

    @pl.loop(2, spectra // 8)
    def _(block):
        for part in range(2):

            def tile(i, part=part):
                return v_ref[part, :, pl.ds(pl.multiple_of((block * 8 + i) * points, points), points)].astype(F32)

            fir(taps, tile, filters, block * 8, stores[part])

    pl.semaphore_wait(pltpu.get_barrier_semaphore(), owners - 1 + 2 * planes + 3)
    rim = (taps - 1) * points
    remote(v_ref.at[:, :, pl.ds((spectra - taps + 1) * points, rim)], rim_ref, rim_send, rim_arrive, later).start()

    @pl.loop(0, stations // 64)
    def _(i):
        first = pl.multiple_of(i * 64, 64)
        station = lax.broadcasted_iota(jnp.int32, (64, stations), 0) + first
        pick_ref[pl.ds(first, 64), :] = jnp.where(order_ref[...] == station, 1.0, 0.0).astype(BF16)

    wait(rim_ref, rim_arrive)
    for block in range(2):
        for part in range(2):

            def tile(i, block=block, part=part):
                t = block * 8 + i
                if t >= 0:
                    return v_ref[part, :, t * points : (t + 1) * points].astype(F32)
                t += taps - 1
                before = rim_ref[part, :, t * points : (t + 1) * points].astype(F32)
                return jnp.where(beam > 0, before, jnp.zeros_like(before))

            fir(taps, tile, filters, block * 8, stores[part])

    fetches[2].wait()
    fetches[3].wait()
    lines = 2 * points
    for i in range(rows):
        at = pl.ds(i, spectra, stride=rows)
        wide = jnp.concatenate([re_ref[at, :], im_ref[at, :]], axis=1)
        high = wide.astype(BF16)
        low = (wide - high.astype(F32)).astype(BF16)
        result = dot(high_ref[...], high, nt) + dot(high_ref[...], low, nt) + dot(low_ref[...], high, nt)
        left_ref[pl.ds(i, lines, stride=rows), :] = result[:, :128]
        right_ref[pl.ds(i, lines, stride=rows), :] = result[:, 128:]

    @pl.loop(0, owners // 4)
    def _(i):
        count = channels * 2 * rows
        for j in range(4):
            at = pl.ds(pl.multiple_of((i * 4 + j) * count, count), count)
            s_ref[i * 4 + j, :, :, :, :128] = left_ref[at, :].astype(BF16).reshape(channels, 2, rows, 128)
            s_ref[i * 4 + j, :, :, :, 128:] = right_ref[at, :].astype(BF16).reshape(channels, 2, rows, 128)

    def entering(at, dx, groups):
        border = (p + 3 + 2 * at) % pairs_count
        for group in groups:
            pair, start = ((p, at), (border, at), (border, 1 - at), (far, 1 - at))[group]
            first = pl.multiple_of((pair * planes + ((x + across - dx) % across) * across) * rows, across * rows)
            yield group, x_ref.at[start * 2 + core, :, :, pl.ds(first, across * rows), :], start

    landing = x_ref.at[mine, :, :, pl.ds(pl.multiple_of(stn * rows, rows), rows), :]
    pltpu.make_async_copy(s_ref.at[stn], landing, arrive.at[0, 0]).start()

    def depart(group, dx, dy):
        pair, entry = ((p, mine), (beyond, mine), (near, others), (far, others))[group]
        owner = pair * planes + ((x + dx) % across) * across + (y + dy) % across
        remote(s_ref.at[owner], landing, send, arrive.at[group, dx], (owner, entry)).start()

    @pl.loop(1, planes)
    def _(i):
        depart(0, i // across, i % across)

    @pl.loop(0, planes)
    def _(i):
        for group in (3, 1, 2):
            depart(group, i // across, i % across)

    def entered(groups, dx):
        for group, block, start in entering(side, dx, groups):
            wait(block, arrive.at[group, dx])
            remote(block, block, forward, forwarded.at[group, dx], partner).start()
            remote(block, block, share.at[start], shared.at[start], sibling).start()

    def passed(groups, dx):
        for group, block, start in entering(1 - side, dx, groups):
            wait(block, forwarded.at[group, dx])
            remote(block, block, share.at[start], shared.at[start], sibling).start()

    half = w_ref.shape[2]

    def weigh(c):
        both = jnp.concatenate([w_ref[0, c], w_ref[1, c]], axis=0)
        for at in range(0, stations, 256):
            turned = dot(both, pick_ref[:, at : at + 256], nn)
            weights_ref[c, :, at : at + 256] = turned.astype(BF16)
            crossed = jnp.concatenate([-turned[half:], turned[:half]], axis=0)
            weights_ref[c, :, stations + at : stations + at + 256] = crossed.astype(BF16)

    @pl.loop(0, across)
    def _(dx):
        entered((0,), dx)

    fetches[4].wait()

    @pl.loop(0, across)
    def _(step):
        entered((2, 1, 3), step)

        @pl.when(step < channels)
        def _():
            weigh(step)

        passed((0,), step)

        @pl.when(step > 0)
        def _():
            passed((2, 1, 3), step - 1)

    passed((2, 1, 3), across - 1)
    for start in range(sides):
        wait(x_ref.at[start * 2 + 1 - core], shared.at[start])

    @pl.loop(0, channels)
    def _(c):
        @pl.loop(0, quarters)
        def _(q):
            result = dot(weights_ref[c, :, :stations], x_ref[q, c, 0], nn)
            result += dot(weights_ref[c, :, stations:], x_ref[q, c, 1], nn)
            for part in range(2):
                beams = result[part * half : (part + 1) * half]
                left_ref[pl.ds(q * 2 + part, half, stride=8), :] = beams[:, :128]
                right_ref[pl.ds(q * 2 + part, half, stride=8), :] = beams[:, 128:]

        for d in range(0, owners, 8):
            at = slice(d * 16, (d + 8) * 16)
            formed_ref[c, d : d + 8, :, :128] = left_ref[at, :].astype(BF16).reshape(8, 16, 128)
            formed_ref[c, d : d + 8, :, 128:] = right_ref[at, :].astype(BF16).reshape(8, 16, 128)

        pltpu.make_async_copy(formed_ref.at[c, stn], got_ref.at[c, stn], beam_arrive.at[c]).start()

        @pl.loop(1, owners)
        def _(i):
            owner = (stn + i) % owners
            remote(formed_ref.at[c, owner], got_ref.at[c, stn], beam_send.at[c], beam_arrive.at[c], (owner, beam)).start()

    count = vis_ref.shape[2]
    start = pl.multiple_of(beam * count, count)
    scale = 1.0 / (quarters * spectra)

    @pl.loop(0, channels)
    def _(c):
        for q in range(quarters):
            at = slice(q * spectra, (q + 1) * spectra)
            for part in range(2):
                for r in range(0, stations, 256):
                    turned_ref[part, r : r + 256, at] = dot(pick_ref[r : r + 256, :], x_ref[q, c, part], nn).astype(BF16)
        real_rows = turned_ref[0, pl.ds(start, count), :]
        imag_rows = turned_ref[1, pl.ds(start, count), :]
        for at in range(0, stations, 256):
            cols = slice(at, at + 256)
            real, imag = turned_ref[0, cols, :], turned_ref[1, cols, :]
            vis_ref[0, c, :, cols] = (dot(real_rows, real, nt) + dot(imag_rows, imag, nt)) * scale
            vis_ref[1, c, :, cols] = (dot(imag_rows, real, nt) - dot(real_rows, imag, nt)) * scale
        pltpu.make_async_copy(vis_ref.at[:, c], vis_hbm.at[:, c], saves.at[c]).start()

    for start in range(sides):
        wait(x_ref.at[start * 2 + core], share.at[start])
    wait(x_ref.at[0], forward)
    wait(s_ref.at[pl.ds(0, owners - 1)], send)
    wait(rim_ref, rim_send)
    for c in range(channels):
        wait(vis_ref.at[:, c], saves.at[c])
        wait(got_ref.at[c], beam_arrive.at[c])
        wait(formed_ref.at[c, pl.ds(0, owners - 1)], beam_send.at[c])


def main(voltages, beam_weights, filter_taps, station_order):
    quarters, owners = lax.axis_size("beam"), lax.axis_size("stn")
    taps, points = filter_taps.shape
    rows, spectra = voltages.shape[1], voltages.shape[2] // points
    channels, half, stations = beam_weights.shape[1:]
    across = 4
    order = np.array([ri * points + c for c in range(points) for ri in range(2)])
    high, low = split(spin_matrix(points).T[order])
    dma = pltpu.SemaphoreType.DMA
    vmem, anywhere = pl.BlockSpec(memory_space=pltpu.VMEM), pl.BlockSpec(memory_space=pl.ANY)
    return pl.pallas_call(
        functools.partial(main_kernel, quarters // 2, across * across, across),
        out_shape=(
            jax.ShapeDtypeStruct((2, channels, stations // quarters, stations), F32),
            jax.ShapeDtypeStruct((channels, owners, 16, spectra), BF16),
        ),
        in_specs=[anywhere] * 5 + [vmem],
        out_specs=(anywhere, anywhere),
        scratch_shapes=[
            pltpu.VMEM(voltages.shape, BF16),
            pltpu.VMEM(beam_weights.shape, BF16),
            pltpu.VMEM(filter_taps.shape, F32),
            pltpu.VMEM(high.shape, BF16),
            pltpu.VMEM(low.shape, BF16),
            pltpu.VMEM((2, rows, (taps - 1) * points), BF16),
            pltpu.VMEM((spectra * rows, points), F32),
            pltpu.VMEM((spectra * rows, points), F32),
            pltpu.VMEM((2 * points * rows, 128), F32),
            pltpu.VMEM((2 * points * rows, 128), F32),
            pltpu.VMEM((owners, channels, 2, rows, spectra), BF16),
            pltpu.VMEM((quarters, channels, 2, stations, spectra), BF16),
            pltpu.VMEM((channels, 2 * half, 2 * stations), BF16),
            pltpu.VMEM((stations, stations), BF16),
            pltpu.VMEM((channels, owners, 16, spectra), BF16),
            pltpu.VMEM((2, stations, quarters * spectra), BF16),
            pltpu.VMEM((2, channels, stations // quarters, stations), F32),
            dma((5,)), dma((channels,)), dma, dma, dma, dma((4, across)), dma, dma((4, across)), dma((2,)), dma((2,)),
            dma((channels,)), dma((channels,)),
        ],
        compiler_params=pltpu.CompilerParams(collective_id=0, has_side_effects=True, vmem_limit_bytes=54 * MIB),
        name="main",
    )(voltages, beam_weights, filter_taps, high, low, station_order.reshape(1, stations))


def tail_kernel(
    taps, quarters, g_ref, vis_ref, taps_ref, high_ref, low_ref, out_ref, kept_ref, held_ref, saved, left_ref, right_ref, *lines
):
    fetch = pltpu.make_async_copy(vis_ref, held_ref, saved.at[0])
    save = pltpu.make_async_copy(held_ref, kept_ref, saved.at[1])
    fetch.start()
    channels = high_ref.shape[0] // 2
    spectra = g_ref.shape[1]
    pad = 16
    left_ref[...] = g_ref[:, :128].astype(F32)
    right_ref[...] = g_ref[:, 128:].astype(F32)
    tn = ((0,), (0,))
    for line in lines:
        line[:pad, :] = jnp.zeros((pad, channels), F32)
    for j in range(2):
        for q in range(quarters):
            parts = [
                jnp.concatenate(
                    [ref[pl.ds(j * 8 + q * 2 + ri, channels, stride=16), :] for ref in (left_ref, right_ref)], axis=1
                )
                for ri in range(2)
            ]
            both = jnp.concatenate(parts, axis=0).astype(BF16)
            result = dot(both, high_ref[...], tn) + dot(both, low_ref[...], tn)
            at = slice(pad + q * spectra, pad + (q + 1) * spectra)
            lines[2 * j][at, :] = result[:, :channels]
            lines[2 * j + 1][at, :] = result[:, channels:]
    fetch.wait()
    save.start()
    block = 64
    weights = [jnp.broadcast_to(taps_ref[m : m + 1, :], (block, channels)) for m in range(taps)]
    for j in range(2):
        for part in range(2):
            line = lines[2 * j + part]
            for t in range(0, quarters * spectra, block):
                total = weights[0] * line[pad + t : pad + t + block, :]
                for m in range(1, taps):
                    total += weights[m] * line[pad + t - m : pad + t - m + block, :]
                out_ref[part, pl.ds(2 * t + j, block, stride=2), :] = total
    save.wait()


def tail(arrived, visibilities, synth_taps, quarters, owners):
    taps, channels = synth_taps.shape
    rows, spectra = arrived.shape
    order = np.arange(2 * channels).reshape(2, owners, channels // owners).transpose(0, 2, 1).reshape(-1)
    high, low = split(spin_matrix(channels).T[order])
    vmem = pl.BlockSpec(memory_space=pltpu.VMEM)
    total = quarters * spectra
    return pl.pallas_call(
        functools.partial(tail_kernel, taps, quarters),
        out_shape=(
            jax.ShapeDtypeStruct((2, 2 * total, channels), F32),
            jax.ShapeDtypeStruct(visibilities.shape, F32),
        ),
        in_specs=[vmem, pl.BlockSpec(memory_space=pl.ANY), vmem, vmem, vmem],
        out_specs=(vmem, pl.BlockSpec(memory_space=pl.ANY)),
        scratch_shapes=[pltpu.VMEM(visibilities.shape, F32), pltpu.SemaphoreType.DMA((2,))]
        + [pltpu.VMEM((rows, 128), F32)] * 2 + [pltpu.VMEM((total + 16, channels), F32)] * 4,
        compiler_params=pltpu.CompilerParams(vmem_limit_bytes=57 * MIB),
        name="tail",
    )(arrived, visibilities, synth_taps, high, low)


def local(voltages, filter_taps, synth_taps, beam_weights, station_order):
    quarters, owners = lax.axis_size("beam"), lax.axis_size("stn")
    channels = filter_taps.shape[1]
    spectra = voltages.shape[2] // channels
    visibilities, arrived = main(voltages, beam_weights, filter_taps, station_order)
    series, visibilities = tail(arrived.reshape(-1, spectra), visibilities, synth_taps, quarters, owners)
    series = series.reshape(2, quarters * spectra, 2, channels).transpose(0, 2, 1, 3)
    return visibilities, series.reshape(2, 1, 2, quarters * spectra * channels)


def solution(mesh):
    in_specs = (P(None, "stn", "beam"), P(), P(), P(None, "stn", "beam", None), P())
    out_specs = (P(None, "stn", "beam", None), P(None, "beam", "stn", None))
    return jax.shard_map(local, mesh=mesh, in_specs=in_specs, out_specs=out_specs, check_vma=False)
```

```python
import functools
import math

import jax
import jax.numpy as jnp
import numpy as np
from jax import lax
from jax.experimental import pallas as pl
from jax.experimental.pallas import tpu as pltpu
from jax.sharding import PartitionSpec as P

F32, BF16 = jnp.float32, jnp.bfloat16
MIB = 2**20


def spin_matrix(points):
    index = np.arange(points)
    angles = (index[:, None] * index[None, :] % points) * (2.0 * math.pi / points)
    cosine, sine = np.cos(angles) / math.sqrt(points), np.sin(angles) / math.sqrt(points)
    upper = np.concatenate([cosine, -sine], axis=1)
    lower = np.concatenate([sine, cosine], axis=1)
    return np.concatenate([upper, lower], axis=0).astype(np.float32)


def split(matrix):
    high = matrix.astype(jnp.bfloat16)
    low = (matrix - high.astype(np.float32)).astype(jnp.bfloat16)
    return jnp.asarray(high), jnp.asarray(low)


def dot(a, b, dims):
    return lax.dot_general(a, b, (dims, ((), ())), preferred_element_type=F32)


MESH = pl.DeviceIdType.MESH


def remote(source, goal, out, into, device):
    return pltpu.make_async_remote_copy(
        src_ref=source, dst_ref=goal, send_sem=out, recv_sem=into, device_id=device, device_id_type=MESH
    )


def wait(ref, sem):
    pltpu.make_async_copy(ref, ref, sem).wait()


def hail(device):
    pl.semaphore_signal(pltpu.get_barrier_semaphore(), inc=1, device_id=device, device_id_type=MESH)


def fir(taps, tile, weights, t0, store):
    step, rows = 8, weights[0].shape[0]
    tiles = [tile(i - (taps - 1)) for i in range(step + taps - 1)]
    for j in range(step):
        total = weights[0] * tiles[j + taps - 1]
        for m in range(1, taps):
            total += weights[m] * tiles[j + taps - 1 - m]
        store[pl.ds((t0 + j) * rows, rows), :] = total


def main_kernel(
    sides, planes, across, v_hbm, w_hbm, taps_hbm, high_hbm, low_hbm, order_ref, vis_hbm, got_ref,
    v_ref, w_ref, taps_ref, high_ref, low_ref, rim_ref, re_ref, im_ref, left_ref, right_ref, s_ref, x_ref, weights_ref,
    pick_ref, formed_ref, turned_ref, vis_ref, loads, saves, rim_send, rim_arrive, send, arrive, forward, forwarded, share, shared,
    beam_send, beam_arrive,
):
    owners = lax.axis_size("stn")
    pairs_count = owners // planes
    stn, beam = lax.axis_index("stn"), lax.axis_index("beam")
    p, place = stn // planes, stn % planes
    x, y = place // across, place % across
    side, core = beam // 2, beam % 2
    channels, quarters, _, stations, spectra = x_ref.shape
    rows = s_ref.shape[3]
    taps, points = taps_ref.shape
    mine, others = side * 2 + core, (1 - side) * 2 + core
    partner, sibling = (stn, others), (stn, side * 2 + 1 - core)
    later, sooner = (stn, (beam + 1) % quarters), (stn, (beam + quarters - 1) % quarters)
    near = (p + 3 + 2 * side) % pairs_count
    far = (p + 2) % pairs_count
    beyond = (p + 1 + 2 * side) % pairs_count
    nn, nt = ((1,), (0,)), ((1,), (1,))

    pieces = ((v_hbm, v_ref), (taps_hbm, taps_ref), (high_hbm, high_ref), (low_hbm, low_ref), (w_hbm, w_ref))
    fetches = [pltpu.make_async_copy(a, b, loads.at[i]) for i, (a, b) in enumerate(pieces)]
    for fetch in fetches:
        fetch.start()

    hail(sibling)
    hail(partner)
    hail(sooner)

    @pl.loop(1, owners)
    def _(i):
        hail(((stn + i) % owners, beam))

    @pl.loop(0, planes)
    def _(i):
        hail((near * planes + i, others))
        hail((far * planes + i, others))

    fetches[0].wait()
    fetches[1].wait()
    filters = [jnp.broadcast_to(taps_ref[m : m + 1, :], (rows, points)) for m in range(taps)]
    stores = (re_ref, im_ref)

    @pl.loop(2, spectra // 8)
    def _(block):
        for part in range(2):

            def tile(i, part=part):
                return v_ref[part, :, pl.ds(pl.multiple_of((block * 8 + i) * points, points), points)].astype(F32)

            fir(taps, tile, filters, block * 8, stores[part])

    pl.semaphore_wait(pltpu.get_barrier_semaphore(), owners - 1 + 2 * planes + 3)
    rim = (taps - 1) * points
    remote(v_ref.at[:, :, pl.ds((spectra - taps + 1) * points, rim)], rim_ref, rim_send, rim_arrive, later).start()

    @pl.loop(0, stations // 64)
    def _(i):
        first = pl.multiple_of(i * 64, 64)
        station = lax.broadcasted_iota(jnp.int32, (64, stations), 0) + first
        pick_ref[pl.ds(first, 64), :] = jnp.where(order_ref[...] == station, 1.0, 0.0).astype(BF16)

    wait(rim_ref, rim_arrive)
    for block in range(2):
        for part in range(2):

            def tile(i, block=block, part=part):
                t = block * 8 + i
                if t >= 0:
                    return v_ref[part, :, t * points : (t + 1) * points].astype(F32)
                t += taps - 1
                before = rim_ref[part, :, t * points : (t + 1) * points].astype(F32)
                return jnp.where(beam > 0, before, jnp.zeros_like(before))

            fir(taps, tile, filters, block * 8, stores[part])

    fetches[2].wait()
    fetches[3].wait()
    lines = 2 * points
    for i in range(rows):
        at = pl.ds(i, spectra, stride=rows)
        wide = jnp.concatenate([re_ref[at, :], im_ref[at, :]], axis=1)
        high = wide.astype(BF16)
        low = (wide - high.astype(F32)).astype(BF16)
        result = dot(high_ref[...], high, nt) + dot(high_ref[...], low, nt) + dot(low_ref[...], high, nt)
        left_ref[pl.ds(i, lines, stride=rows), :] = result[:, :128]
        right_ref[pl.ds(i, lines, stride=rows), :] = result[:, 128:]

    def settle(c):
        @pl.loop(0, owners // 8)
        def _(i):
            count = 2 * rows
            for j in range(8):
                at = pl.ds(pl.multiple_of((c * owners + i * 8 + j) * count, count), count)
                s_ref[c, i * 8 + j, :, :, :128] = left_ref[at, :].astype(BF16).reshape(2, rows, 128)
                s_ref[c, i * 8 + j, :, :, 128:] = right_ref[at, :].astype(BF16).reshape(2, rows, 128)

    def entering(c, at, dx, groups):
        border = (p + 3 + 2 * at) % pairs_count
        for group in groups:
            pair, start = ((p, at), (border, at), (border, 1 - at), (far, 1 - at))[group]
            first = pl.multiple_of((pair * planes + ((x + across - dx) % across) * across) * rows, across * rows)
            yield group, x_ref.at[c, start * 2 + core, :, pl.ds(first, across * rows), :], start

    def landing(c):
        return x_ref.at[c, mine, :, pl.ds(pl.multiple_of(stn * rows, rows), rows), :]

    def stay(c):
        pltpu.make_async_copy(s_ref.at[c, stn], landing(c), arrive.at[c, 0, 0]).start()

    def depart(c, group, dx, dy):
        pair, entry = ((p, mine), (beyond, mine), (near, others), (far, others))[group]
        owner = pair * planes + ((x + dx) % across) * across + (y + dy) % across
        remote(s_ref.at[c, owner], landing(c), send.at[c], arrive.at[c, group, dx], (owner, entry)).start()

    def entered(c, groups, dx):
        for group, block, start in entering(c, side, dx, groups):
            wait(block, arrive.at[c, group, dx])
            remote(block, block, forward.at[c], forwarded.at[c, group, dx], partner).start()
            remote(block, block, share.at[c, start], shared.at[c, start], sibling).start()

    def passed(c, groups, dx):
        for group, block, start in entering(c, 1 - side, dx, groups):
            wait(block, forwarded.at[c, group, dx])
            remote(block, block, share.at[c, start], shared.at[c, start], sibling).start()

    half = w_ref.shape[2]

    def weigh(c):
        both = jnp.concatenate([w_ref[0, c], w_ref[1, c]], axis=0)
        for at in range(0, stations, 256):
            turned = dot(both, pick_ref[:, at : at + 256], nn)
            weights_ref[c, :, at : at + 256] = turned.astype(BF16)
            crossed = jnp.concatenate([-turned[half:], turned[:half]], axis=0)
            weights_ref[c, :, stations + at : stations + at + 256] = crossed.astype(BF16)

    def beams(c):
        for start in range(sides):
            wait(x_ref.at[c, start * 2 + 1 - core], shared.at[c, start])

        @pl.loop(0, quarters)
        def _(q):
            result = dot(weights_ref[c, :, :stations], x_ref[c, q, 0], nn)
            result += dot(weights_ref[c, :, stations:], x_ref[c, q, 1], nn)
            for part in range(2):
                formed = result[part * half : (part + 1) * half]
                left_ref[pl.ds(q * 2 + part, half, stride=8), :] = formed[:, :128]
                right_ref[pl.ds(q * 2 + part, half, stride=8), :] = formed[:, 128:]

        for d in range(0, owners, 8):
            at = slice(d * 16, (d + 8) * 16)
            formed_ref[c, d : d + 8, :, :128] = left_ref[at, :].astype(BF16).reshape(8, 16, 128)
            formed_ref[c, d : d + 8, :, 128:] = right_ref[at, :].astype(BF16).reshape(8, 16, 128)

        pltpu.make_async_copy(formed_ref.at[c, stn], got_ref.at[c, stn], beam_arrive.at[c]).start()

        def dispatch(owner):
            remote(formed_ref.at[c, owner], got_ref.at[c, stn], beam_send.at[c], beam_arrive.at[c], (owner, beam)).start()

        @pl.loop(0, planes)
        def _(i):
            for pair in (far, near, beyond):
                dispatch(pair * planes + (place + i) % planes)

            @pl.when(i > 0)
            def _():
                dispatch(p * planes + (place + i) % planes)

    count = vis_ref.shape[2]
    first_row = pl.multiple_of(beam * count, count)
    scale = 1.0 / (quarters * spectra)

    def arrange(c, some):
        for q in some:
            at = slice(q * spectra, (q + 1) * spectra)
            for part in range(2):
                for r in range(0, stations, 256):
                    turned_ref[part, r : r + 256, at] = dot(pick_ref[r : r + 256, :], x_ref[c, q, part], nn).astype(BF16)

    def correlate(c):
        real_rows = turned_ref[0, pl.ds(first_row, count), :]
        imag_rows = turned_ref[1, pl.ds(first_row, count), :]
        for at in range(0, stations, 256):
            cols = slice(at, at + 256)
            real, imag = turned_ref[0, cols, :], turned_ref[1, cols, :]
            vis_ref[0, c, :, cols] = (dot(real_rows, real, nt) + dot(imag_rows, imag, nt)) * scale
            vis_ref[1, c, :, cols] = (dot(imag_rows, real, nt) - dot(real_rows, imag, nt)) * scale
        pltpu.make_async_copy(vis_ref.at[:, c], vis_hbm.at[:, c], saves.at[c]).start()

    outer = (2, 1, 3)
    last = across - 1
    settle(0)
    stay(0)

    @pl.loop(1, planes)
    def _(i):
        depart(0, 0, i // across, i % across)

    @pl.loop(0, planes)
    def _(i):
        for group in (3, 1, 2):
            depart(0, group, i // across, i % across)

    settle(1)

    @pl.loop(0, across)
    def _(dx):
        entered(0, (0,), dx)

    fetches[4].wait()
    stay(1)

    @pl.loop(0, across)
    def _(step):
        entered(0, outer, step)

        @pl.loop(0, across)
        def _(dy):
            @pl.when((step > 0) | (dy > 0))
            def _():
                depart(1, 0, step, dy)

            for group in (3, 1, 2):
                depart(1, group, step, dy)

        @pl.when(step < channels)
        def _():
            weigh(step)

        passed(0, (0,), step)

        @pl.when(step > 0)
        def _():
            passed(0, outer, step - 1)

    @pl.loop(0, across)
    def _(dx):
        entered(1, (0,), dx)

    passed(0, outer, last)
    beams(0)
    entered(1, outer, 0)
    passed(1, (0,), 0)
    arrange(0, (0, 1))
    entered(1, outer, 1)
    passed(1, (0,), 1)
    passed(1, outer, 0)
    arrange(0, (2, 3))
    entered(1, outer, 2)
    passed(1, (0,), 2)
    passed(1, outer, 1)
    correlate(0)
    entered(1, outer, 3)
    passed(1, (0,), 3)
    passed(1, outer, 2)
    passed(1, outer, 3)
    beams(1)
    arrange(1, range(quarters))
    correlate(1)

    wait(rim_ref, rim_send)
    for c in range(channels):
        for start in range(sides):
            wait(x_ref.at[c, start * 2 + core], share.at[c, start])
        wait(x_ref.at[c, 0], forward.at[c])
        wait(s_ref.at[c, pl.ds(0, owners - 1)], send.at[c])
        wait(formed_ref.at[c, pl.ds(0, owners - 1)], beam_send.at[c])
        wait(vis_ref.at[:, c], saves.at[c])
        wait(got_ref.at[c], beam_arrive.at[c])


def main(voltages, beam_weights, filter_taps, station_order):
    quarters, owners = lax.axis_size("beam"), lax.axis_size("stn")
    taps, points = filter_taps.shape
    rows, spectra = voltages.shape[1], voltages.shape[2] // points
    channels, half, stations = beam_weights.shape[1:]
    across = 4
    order = np.arange(2 * points).reshape(2, owners, channels).transpose(2, 1, 0).reshape(-1)
    high, low = split(spin_matrix(points).T[order])
    dma = pltpu.SemaphoreType.DMA
    vmem, anywhere = pl.BlockSpec(memory_space=pltpu.VMEM), pl.BlockSpec(memory_space=pl.ANY)
    return pl.pallas_call(
        functools.partial(main_kernel, quarters // 2, across * across, across),
        out_shape=(
            jax.ShapeDtypeStruct((2, channels, stations // quarters, stations), F32),
            jax.ShapeDtypeStruct((channels, owners, 16, spectra), BF16),
        ),
        in_specs=[anywhere] * 5 + [vmem],
        out_specs=(anywhere, anywhere),
        scratch_shapes=[
            pltpu.VMEM(voltages.shape, BF16),
            pltpu.VMEM(beam_weights.shape, BF16),
            pltpu.VMEM(filter_taps.shape, F32),
            pltpu.VMEM(high.shape, BF16),
            pltpu.VMEM(low.shape, BF16),
            pltpu.VMEM((2, rows, (taps - 1) * points), BF16),
            pltpu.VMEM((spectra * rows, points), F32),
            pltpu.VMEM((spectra * rows, points), F32),
            pltpu.VMEM((2 * points * rows, 128), F32),
            pltpu.VMEM((2 * points * rows, 128), F32),
            pltpu.VMEM((channels, owners, 2, rows, spectra), BF16),
            pltpu.VMEM((channels, quarters, 2, stations, spectra), BF16),
            pltpu.VMEM((channels, 2 * half, 2 * stations), BF16),
            pltpu.VMEM((stations, stations), BF16),
            pltpu.VMEM((channels, owners, 16, spectra), BF16),
            pltpu.VMEM((2, stations, quarters * spectra), BF16),
            pltpu.VMEM((2, channels, stations // quarters, stations), F32),
            dma((5,)), dma((channels,)), dma, dma,
            dma((channels,)), dma((channels, 4, across)), dma((channels,)), dma((channels, 4, across)),
            dma((channels, 2)), dma((channels, 2)),
            dma((channels,)), dma((channels,)),
        ],
        compiler_params=pltpu.CompilerParams(collective_id=0, has_side_effects=True, vmem_limit_bytes=54 * MIB),
        name="main",
    )(voltages, beam_weights, filter_taps, high, low, station_order.reshape(1, stations))


def tail_kernel(
    taps, quarters, g_ref, vis_ref, taps_ref, high_ref, low_ref, out_ref, kept_ref, held_ref, saved, left_ref, right_ref, *lines
):
    pieces = [(i, c) for i in range(2) for c in range(vis_ref.shape[1])]
    fetches = [pltpu.make_async_copy(vis_ref.at[i], held_ref.at[i], saved.at[0, n]) for n, i in enumerate(pieces)]
    saves = [pltpu.make_async_copy(held_ref.at[i], kept_ref.at[i], saved.at[1, n]) for n, i in enumerate(pieces)]
    for fetch in fetches:
        fetch.start()
    channels = high_ref.shape[0] // 2
    spectra = g_ref.shape[1]
    pad = 16
    left_ref[...] = g_ref[:, :128].astype(F32)
    right_ref[...] = g_ref[:, 128:].astype(F32)
    tn = ((0,), (0,))
    for line in lines:
        line[:pad, :] = jnp.zeros((pad, channels), F32)
    for j in range(2):
        for q in range(quarters):
            parts = [
                jnp.concatenate(
                    [ref[pl.ds(j * 8 + q * 2 + ri, channels, stride=16), :] for ref in (left_ref, right_ref)], axis=1
                )
                for ri in range(2)
            ]
            both = jnp.concatenate(parts, axis=0).astype(BF16)
            result = dot(both, high_ref[...], tn) + dot(both, low_ref[...], tn)
            at = slice(pad + q * spectra, pad + (q + 1) * spectra)
            lines[2 * j][at, :] = result[:, :channels]
            lines[2 * j + 1][at, :] = result[:, channels:]
    for fetch, save in zip(fetches, saves):
        fetch.wait()
        save.start()
    block = 64
    weights = [jnp.broadcast_to(taps_ref[m : m + 1, :], (block, channels)) for m in range(taps)]
    for j in range(2):
        for part in range(2):
            line = lines[2 * j + part]
            for t in range(0, quarters * spectra, block):
                total = weights[0] * line[pad + t : pad + t + block, :]
                for m in range(1, taps):
                    total += weights[m] * line[pad + t - m : pad + t - m + block, :]
                out_ref[part, pl.ds(2 * t + j, block, stride=2), :] = total
    for save in saves:
        save.wait()


def tail(arrived, visibilities, synth_taps, quarters, owners):
    taps, channels = synth_taps.shape
    rows, spectra = arrived.shape
    order = np.arange(2 * channels).reshape(2, owners, channels // owners).transpose(0, 2, 1).reshape(-1)
    high, low = split(spin_matrix(channels).T[order])
    vmem = pl.BlockSpec(memory_space=pltpu.VMEM)
    total = quarters * spectra
    return pl.pallas_call(
        functools.partial(tail_kernel, taps, quarters),
        out_shape=(
            jax.ShapeDtypeStruct((2, 2 * total, channels), F32),
            jax.ShapeDtypeStruct(visibilities.shape, F32),
        ),
        in_specs=[vmem, pl.BlockSpec(memory_space=pl.ANY), vmem, vmem, vmem],
        out_specs=(vmem, pl.BlockSpec(memory_space=pl.ANY)),
        scratch_shapes=[pltpu.VMEM(visibilities.shape, F32), pltpu.SemaphoreType.DMA((2, 4))]
        + [pltpu.VMEM((rows, 128), F32)] * 2 + [pltpu.VMEM((total + 16, channels), F32)] * 4,
        compiler_params=pltpu.CompilerParams(vmem_limit_bytes=57 * MIB),
        name="tail",
    )(arrived, visibilities, synth_taps, high, low)


def local(voltages, filter_taps, synth_taps, beam_weights, station_order):
    quarters, owners = lax.axis_size("beam"), lax.axis_size("stn")
    channels = filter_taps.shape[1]
    spectra = voltages.shape[2] // channels
    visibilities, arrived = main(voltages, beam_weights, filter_taps, station_order)
    series, visibilities = tail(arrived.reshape(-1, spectra), visibilities, synth_taps, quarters, owners)
    series = series.reshape(2, quarters * spectra, 2, channels).transpose(0, 2, 1, 3)
    return visibilities, series.reshape(2, 1, 2, quarters * spectra * channels)


def solution(mesh):
    in_specs = (P(None, "stn", "beam"), P(), P(), P(None, "stn", "beam", None), P())
    out_specs = (P(None, "stn", "beam", None), P(None, "beam", "stn", None))
    return jax.shard_map(local, mesh=mesh, in_specs=in_specs, out_specs=out_specs, check_vma=False)
```

```python
import functools
import math

import jax
import jax.numpy as jnp
import numpy as np
from jax import lax
from jax.experimental import pallas as pl
from jax.experimental.pallas import tpu as pltpu
from jax.sharding import PartitionSpec as P

F32, BF16 = jnp.float32, jnp.bfloat16
MIB = 2**20


def spin_matrix(points):
    index = np.arange(points)
    angles = (index[:, None] * index[None, :] % points) * (2.0 * math.pi / points)
    cosine, sine = np.cos(angles) / math.sqrt(points), np.sin(angles) / math.sqrt(points)
    upper = np.concatenate([cosine, -sine], axis=1)
    lower = np.concatenate([sine, cosine], axis=1)
    return np.concatenate([upper, lower], axis=0).astype(np.float32)


def split(matrix):
    high = matrix.astype(jnp.bfloat16)
    low = (matrix - high.astype(np.float32)).astype(jnp.bfloat16)
    return jnp.asarray(high), jnp.asarray(low)


def dot(a, b, dims):
    return lax.dot_general(a, b, (dims, ((), ())), preferred_element_type=F32)


MESH = pl.DeviceIdType.MESH


def remote(source, goal, out, into, device):
    return pltpu.make_async_remote_copy(
        src_ref=source, dst_ref=goal, send_sem=out, recv_sem=into, device_id=device, device_id_type=MESH
    )


def wait(ref, sem):
    pltpu.make_async_copy(ref, ref, sem).wait()


def hail(device):
    pl.semaphore_signal(pltpu.get_barrier_semaphore(), inc=1, device_id=device, device_id_type=MESH)


def fir(taps, tile, weights, t0, store):
    step, rows = 8, weights[0].shape[0]
    tiles = [tile(i - (taps - 1)) for i in range(step + taps - 1)]
    for j in range(step):
        total = weights[0] * tiles[j + taps - 1]
        for m in range(1, taps):
            total += weights[m] * tiles[j + taps - 1 - m]
        store[pl.ds((t0 + j) * rows, rows), :] = total


def main_kernel(
    sides, planes, across, v_hbm, w_hbm, taps_hbm, high_hbm, low_hbm, order_ref, vis_hbm, got_ref,
    v_ref, w_ref, taps_ref, high_ref, low_ref, rim_ref, re_ref, im_ref, left_ref, right_ref, s_ref, x_ref, weights_ref,
    pick_ref, formed_ref, turned_ref, vis_ref, loads, saves, rim_send, rim_arrive, send, arrive, forward, forwarded, share, shared,
    beam_send, beam_arrive,
):
    owners = lax.axis_size("stn")
    pairs_count = owners // planes
    stn, beam = lax.axis_index("stn"), lax.axis_index("beam")
    p, place = stn // planes, stn % planes
    x, y = place // across, place % across
    side, core = beam // 2, beam % 2
    channels, quarters, _, stations, spectra = x_ref.shape
    rows = s_ref.shape[3]
    taps, points = taps_ref.shape
    mine, others = side * 2 + core, (1 - side) * 2 + core
    partner, sibling = (stn, others), (stn, side * 2 + 1 - core)
    later, sooner = (stn, (beam + 1) % quarters), (stn, (beam + quarters - 1) % quarters)
    near = (p + 3 + 2 * side) % pairs_count
    far = (p + 2) % pairs_count
    beyond = (p + 1 + 2 * side) % pairs_count
    nn, nt = ((1,), (0,)), ((1,), (1,))

    pieces = ((v_hbm, v_ref), (taps_hbm, taps_ref), (high_hbm, high_ref), (low_hbm, low_ref), (w_hbm, w_ref))
    fetches = [pltpu.make_async_copy(a, b, loads.at[i]) for i, (a, b) in enumerate(pieces)]
    for fetch in fetches:
        fetch.start()

    hail(sibling)
    hail(partner)
    hail(sooner)

    @pl.loop(1, owners)
    def _(i):
        hail(((stn + i) % owners, beam))

    @pl.loop(0, planes)
    def _(i):
        hail((near * planes + i, others))
        hail((far * planes + i, others))

    fetches[0].wait()
    fetches[1].wait()
    filters = [jnp.broadcast_to(taps_ref[m : m + 1, :], (rows, points)) for m in range(taps)]
    stores = (re_ref, im_ref)

    def inner(first, end):
        @pl.loop(first, end)
        def _(block):
            for part in range(2):

                def tile(i, part=part):
                    return v_ref[part, :, pl.ds(pl.multiple_of((block * 8 + i) * points, points), points)].astype(F32)

                fir(taps, tile, filters, block * 8, stores[part])

    blocks = spectra // 8
    inner(2, blocks // 2)
    pl.semaphore_wait(pltpu.get_barrier_semaphore(), owners - 1 + 2 * planes + 3)
    rim = (taps - 1) * points
    remote(v_ref.at[:, :, pl.ds((spectra - taps + 1) * points, rim)], rim_ref, rim_send, rim_arrive, later).start()

    inner(blocks // 2, blocks)
    wait(rim_ref, rim_arrive)
    for block in range(2):
        for part in range(2):

            def tile(i, block=block, part=part):
                t = block * 8 + i
                if t >= 0:
                    return v_ref[part, :, t * points : (t + 1) * points].astype(F32)
                t += taps - 1
                before = rim_ref[part, :, t * points : (t + 1) * points].astype(F32)
                return jnp.where(beam > 0, before, jnp.zeros_like(before))

            fir(taps, tile, filters, block * 8, stores[part])

    fetches[2].wait()
    fetches[3].wait()
    def transform(c):
        lines = 2 * owners
        cut = slice(c * lines, (c + 1) * lines)
        for i in range(rows):
            at = pl.ds(i, spectra, stride=rows)
            wide = jnp.concatenate([re_ref[at, :], im_ref[at, :]], axis=1)
            high = wide.astype(BF16)
            low = (wide - high.astype(F32)).astype(BF16)
            result = dot(high_ref[cut, :], high, nt) + dot(high_ref[cut, :], low, nt) + dot(low_ref[cut, :], high, nt)
            left_ref[pl.ds(c * lines * rows + i, lines, stride=rows), :] = result[:, :128]
            right_ref[pl.ds(c * lines * rows + i, lines, stride=rows), :] = result[:, 128:]

    def settle(c):
        @pl.loop(0, owners // 8)
        def _(i):
            count = 2 * rows
            for j in range(8):
                at = pl.ds(pl.multiple_of((c * owners + i * 8 + j) * count, count), count)
                s_ref[c, i * 8 + j, :, :, :128] = left_ref[at, :].astype(BF16).reshape(2, rows, 128)
                s_ref[c, i * 8 + j, :, :, 128:] = right_ref[at, :].astype(BF16).reshape(2, rows, 128)

    def entering(c, at, dx, groups):
        border = (p + 3 + 2 * at) % pairs_count
        for group in groups:
            pair, start = ((p, at), (border, at), (border, 1 - at), (far, 1 - at))[group]
            first = pl.multiple_of((pair * planes + ((x + across - dx) % across) * across) * rows, across * rows)
            yield group, x_ref.at[c, start * 2 + core, :, pl.ds(first, across * rows), :], start

    def landing(c):
        return x_ref.at[c, mine, :, pl.ds(pl.multiple_of(stn * rows, rows), rows), :]

    def stay(c):
        pltpu.make_async_copy(s_ref.at[c, stn], landing(c), arrive.at[c, 0, 0]).start()

    def depart(c, group, dx, dy):
        pair, entry = ((p, mine), (beyond, mine), (near, others), (far, others))[group]
        owner = pair * planes + ((x + dx) % across) * across + (y + dy) % across
        remote(s_ref.at[c, owner], landing(c), send.at[c], arrive.at[c, group, dx], (owner, entry)).start()

    def entered(c, groups, dx):
        for group, block, start in entering(c, side, dx, groups):
            wait(block, arrive.at[c, group, dx])
            remote(block, block, forward.at[c], forwarded.at[c, group, dx], partner).start()
            remote(block, block, share.at[c, start], shared.at[c, start], sibling).start()

    def passed(c, groups, dx):
        for group, block, start in entering(c, 1 - side, dx, groups):
            wait(block, forwarded.at[c, group, dx])
            remote(block, block, share.at[c, start], shared.at[c, start], sibling).start()

    half = w_ref.shape[2]

    def weigh(c):
        both = jnp.concatenate([w_ref[0, c], w_ref[1, c]], axis=0)
        for at in range(0, stations, 256):
            turned = dot(both, pick_ref[:, at : at + 256], nn)
            weights_ref[c, :, at : at + 256] = turned.astype(BF16)
            crossed = jnp.concatenate([-turned[half:], turned[:half]], axis=0)
            weights_ref[c, :, stations + at : stations + at + 256] = crossed.astype(BF16)

    def beams(c):
        for start in range(sides):
            wait(x_ref.at[c, start * 2 + 1 - core], shared.at[c, start])

        @pl.loop(0, quarters)
        def _(q):
            result = dot(weights_ref[c, :, :stations], x_ref[c, q, 0], nn)
            result += dot(weights_ref[c, :, stations:], x_ref[c, q, 1], nn)
            for part in range(2):
                formed = result[part * half : (part + 1) * half]
                left_ref[pl.ds(q * 2 + part, half, stride=8), :] = formed[:, :128]
                right_ref[pl.ds(q * 2 + part, half, stride=8), :] = formed[:, 128:]

        for d in range(0, owners, 8):
            at = slice(d * 16, (d + 8) * 16)
            formed_ref[c, d : d + 8, :, :128] = left_ref[at, :].astype(BF16).reshape(8, 16, 128)
            formed_ref[c, d : d + 8, :, 128:] = right_ref[at, :].astype(BF16).reshape(8, 16, 128)

        pltpu.make_async_copy(formed_ref.at[c, stn], got_ref.at[c, stn], beam_arrive.at[c]).start()

        def dispatch(owner):
            remote(formed_ref.at[c, owner], got_ref.at[c, stn], beam_send.at[c], beam_arrive.at[c], (owner, beam)).start()

        @pl.loop(0, planes)
        def _(i):
            for pair in (far, near, beyond):
                dispatch(pair * planes + (place + i) % planes)

            @pl.when(i > 0)
            def _():
                dispatch(p * planes + (place + i) % planes)

    count = vis_ref.shape[2]
    first_row = pl.multiple_of(beam * count, count)
    scale = 1.0 / (quarters * spectra)

    def arrange(c, some):
        for q in some:
            at = slice(q * spectra, (q + 1) * spectra)
            for part in range(2):
                for r in range(0, stations, 256):
                    turned_ref[part, r : r + 256, at] = dot(pick_ref[r : r + 256, :], x_ref[c, q, part], nn).astype(BF16)

    def correlate(c):
        real_rows = turned_ref[0, pl.ds(first_row, count), :]
        imag_rows = turned_ref[1, pl.ds(first_row, count), :]
        for at in range(0, stations, 256):
            cols = slice(at, at + 256)
            real, imag = turned_ref[0, cols, :], turned_ref[1, cols, :]
            vis_ref[0, c, :, cols] = (dot(real_rows, real, nt) + dot(imag_rows, imag, nt)) * scale
            vis_ref[1, c, :, cols] = (dot(imag_rows, real, nt) - dot(real_rows, imag, nt)) * scale
        pltpu.make_async_copy(vis_ref.at[:, c], vis_hbm.at[:, c], saves.at[c]).start()

    outer = (2, 1, 3)
    last = across - 1
    transform(0)
    settle(0)
    stay(0)

    @pl.loop(1, planes)
    def _(i):
        depart(0, 0, i // across, i % across)

    @pl.loop(0, planes)
    def _(i):
        for group in (3, 1, 2):
            depart(0, group, i // across, i % across)

    transform(1)
    settle(1)

    @pl.loop(0, across)
    def _(dx):
        entered(0, (0,), dx)

    @pl.loop(0, stations // 64)
    def _(i):
        first = pl.multiple_of(i * 64, 64)
        station = lax.broadcasted_iota(jnp.int32, (64, stations), 0) + first
        pick_ref[pl.ds(first, 64), :] = jnp.where(order_ref[...] == station, 1.0, 0.0).astype(BF16)

    fetches[4].wait()
    stay(1)

    @pl.loop(0, across)
    def _(step):
        entered(0, outer, step)

        @pl.loop(0, across)
        def _(dy):
            @pl.when((step > 0) | (dy > 0))
            def _():
                depart(1, 0, step, dy)

            for group in (3, 1, 2):
                depart(1, group, step, dy)

        @pl.when(step < channels)
        def _():
            weigh(step)

        passed(0, (0,), step)

        @pl.when(step > 0)
        def _():
            passed(0, outer, step - 1)

    @pl.loop(0, across)
    def _(dx):
        entered(1, (0,), dx)

    passed(0, outer, last)
    beams(0)
    entered(1, outer, 0)
    passed(1, (0,), 0)
    arrange(0, (0, 1))
    entered(1, outer, 1)
    passed(1, (0,), 1)
    passed(1, outer, 0)
    arrange(0, (2, 3))
    entered(1, outer, 2)
    passed(1, (0,), 2)
    passed(1, outer, 1)
    correlate(0)
    entered(1, outer, 3)
    passed(1, (0,), 3)
    passed(1, outer, 2)
    passed(1, outer, 3)
    beams(1)
    arrange(1, range(quarters))
    correlate(1)

    wait(rim_ref, rim_send)
    for c in range(channels):
        for start in range(sides):
            wait(x_ref.at[c, start * 2 + core], share.at[c, start])
        wait(x_ref.at[c, 0], forward.at[c])
        wait(s_ref.at[c, pl.ds(0, owners - 1)], send.at[c])
        wait(formed_ref.at[c, pl.ds(0, owners - 1)], beam_send.at[c])
        wait(vis_ref.at[:, c], saves.at[c])
        wait(got_ref.at[c], beam_arrive.at[c])


def main(voltages, beam_weights, filter_taps, station_order):
    quarters, owners = lax.axis_size("beam"), lax.axis_size("stn")
    taps, points = filter_taps.shape
    rows, spectra = voltages.shape[1], voltages.shape[2] // points
    channels, half, stations = beam_weights.shape[1:]
    across = 4
    order = np.arange(2 * points).reshape(2, owners, channels).transpose(2, 1, 0).reshape(-1)
    high, low = split(spin_matrix(points).T[order])
    dma = pltpu.SemaphoreType.DMA
    vmem, anywhere = pl.BlockSpec(memory_space=pltpu.VMEM), pl.BlockSpec(memory_space=pl.ANY)
    return pl.pallas_call(
        functools.partial(main_kernel, quarters // 2, across * across, across),
        out_shape=(
            jax.ShapeDtypeStruct((2, channels, stations // quarters, stations), F32),
            jax.ShapeDtypeStruct((channels, owners, 16, spectra), BF16),
        ),
        in_specs=[anywhere] * 5 + [vmem],
        out_specs=(anywhere, anywhere),
        scratch_shapes=[
            pltpu.VMEM(voltages.shape, BF16),
            pltpu.VMEM(beam_weights.shape, BF16),
            pltpu.VMEM(filter_taps.shape, F32),
            pltpu.VMEM(high.shape, BF16),
            pltpu.VMEM(low.shape, BF16),
            pltpu.VMEM((2, rows, (taps - 1) * points), BF16),
            pltpu.VMEM((spectra * rows, points), F32),
            pltpu.VMEM((spectra * rows, points), F32),
            pltpu.VMEM((2 * points * rows, 128), F32),
            pltpu.VMEM((2 * points * rows, 128), F32),
            pltpu.VMEM((channels, owners, 2, rows, spectra), BF16),
            pltpu.VMEM((channels, quarters, 2, stations, spectra), BF16),
            pltpu.VMEM((channels, 2 * half, 2 * stations), BF16),
            pltpu.VMEM((stations, stations), BF16),
            pltpu.VMEM((channels, owners, 16, spectra), BF16),
            pltpu.VMEM((2, stations, quarters * spectra), BF16),
            pltpu.VMEM((2, channels, stations // quarters, stations), F32),
            dma((5,)), dma((channels,)), dma, dma,
            dma((channels,)), dma((channels, 4, across)), dma((channels,)), dma((channels, 4, across)),
            dma((channels, 2)), dma((channels, 2)),
            dma((channels,)), dma((channels,)),
        ],
        compiler_params=pltpu.CompilerParams(collective_id=0, has_side_effects=True, vmem_limit_bytes=54 * MIB),
        name="main",
    )(voltages, beam_weights, filter_taps, high, low, station_order.reshape(1, stations))


def tail_kernel(
    taps, quarters, g_ref, vis_ref, taps_ref, high_ref, low_ref, out_ref, kept_ref, held_ref, saved, left_ref, right_ref, *lines
):
    pieces = [(i, c) for i in range(2) for c in range(vis_ref.shape[1])]
    fetches = [pltpu.make_async_copy(vis_ref.at[i], held_ref.at[i], saved.at[0, n]) for n, i in enumerate(pieces)]
    saves = [pltpu.make_async_copy(held_ref.at[i], kept_ref.at[i], saved.at[1, n]) for n, i in enumerate(pieces)]
    for fetch in fetches:
        fetch.start()
    channels = high_ref.shape[0] // 2
    spectra = g_ref.shape[1]
    pad = 16
    left_ref[...] = g_ref[:, :128].astype(F32)
    right_ref[...] = g_ref[:, 128:].astype(F32)
    tn = ((0,), (0,))
    for line in lines:
        line[:pad, :] = jnp.zeros((pad, channels), F32)
    for j in range(2):
        for q in range(quarters):
            parts = [
                jnp.concatenate(
                    [ref[pl.ds(j * 8 + q * 2 + ri, channels, stride=16), :] for ref in (left_ref, right_ref)], axis=1
                )
                for ri in range(2)
            ]
            both = jnp.concatenate(parts, axis=0).astype(BF16)
            result = dot(both, high_ref[...], tn) + dot(both, low_ref[...], tn)
            at = slice(pad + q * spectra, pad + (q + 1) * spectra)
            lines[2 * j][at, :] = result[:, :channels]
            lines[2 * j + 1][at, :] = result[:, channels:]
    for fetch, save in zip(fetches, saves):
        fetch.wait()
        save.start()
    block = 64
    weights = [jnp.broadcast_to(taps_ref[m : m + 1, :], (block, channels)) for m in range(taps)]
    for j in range(2):
        for part in range(2):
            line = lines[2 * j + part]
            for t in range(0, quarters * spectra, block):
                total = weights[0] * line[pad + t : pad + t + block, :]
                for m in range(1, taps):
                    total += weights[m] * line[pad + t - m : pad + t - m + block, :]
                out_ref[part, pl.ds(2 * t + j, block, stride=2), :] = total
    for save in saves:
        save.wait()


def tail(arrived, visibilities, synth_taps, quarters, owners):
    taps, channels = synth_taps.shape
    rows, spectra = arrived.shape
    order = np.arange(2 * channels).reshape(2, owners, channels // owners).transpose(0, 2, 1).reshape(-1)
    high, low = split(spin_matrix(channels).T[order])
    vmem = pl.BlockSpec(memory_space=pltpu.VMEM)
    total = quarters * spectra
    return pl.pallas_call(
        functools.partial(tail_kernel, taps, quarters),
        out_shape=(
            jax.ShapeDtypeStruct((2, 2 * total, channels), F32),
            jax.ShapeDtypeStruct(visibilities.shape, F32),
        ),
        in_specs=[vmem, pl.BlockSpec(memory_space=pl.ANY), vmem, vmem, vmem],
        out_specs=(vmem, pl.BlockSpec(memory_space=pl.ANY)),
        scratch_shapes=[pltpu.VMEM(visibilities.shape, F32), pltpu.SemaphoreType.DMA((2, 4))]
        + [pltpu.VMEM((rows, 128), F32)] * 2 + [pltpu.VMEM((total + 16, channels), F32)] * 4,
        compiler_params=pltpu.CompilerParams(vmem_limit_bytes=57 * MIB),
        name="tail",
    )(arrived, visibilities, synth_taps, high, low)


def local(voltages, filter_taps, synth_taps, beam_weights, station_order):
    quarters, owners = lax.axis_size("beam"), lax.axis_size("stn")
    channels = filter_taps.shape[1]
    spectra = voltages.shape[2] // channels
    visibilities, arrived = main(voltages, beam_weights, filter_taps, station_order)
    series, visibilities = tail(arrived.reshape(-1, spectra), visibilities, synth_taps, quarters, owners)
    series = series.reshape(2, quarters * spectra, 2, channels).transpose(0, 2, 1, 3)
    return visibilities, series.reshape(2, 1, 2, quarters * spectra * channels)


def solution(mesh):
    in_specs = (P(None, "stn", "beam"), P(), P(), P(None, "stn", "beam", None), P())
    out_specs = (P(None, "stn", "beam", None), P(None, "beam", "stn", None))
    return jax.shard_map(local, mesh=mesh, in_specs=in_specs, out_specs=out_specs, check_vma=False)
```

```python
import functools
import math

import jax
import jax.numpy as jnp
import numpy as np
from jax import lax
from jax.experimental import pallas as pl
from jax.experimental.pallas import tpu as pltpu
from jax.sharding import PartitionSpec as P

F32, BF16 = jnp.float32, jnp.bfloat16
MIB = 2**20


def spin_matrix(points):
    index = np.arange(points)
    angles = (index[:, None] * index[None, :] % points) * (2.0 * math.pi / points)
    cosine, sine = np.cos(angles) / math.sqrt(points), np.sin(angles) / math.sqrt(points)
    upper = np.concatenate([cosine, -sine], axis=1)
    lower = np.concatenate([sine, cosine], axis=1)
    return np.concatenate([upper, lower], axis=0).astype(np.float32)


def split(matrix):
    high = matrix.astype(jnp.bfloat16)
    low = (matrix - high.astype(np.float32)).astype(jnp.bfloat16)
    return jnp.asarray(high), jnp.asarray(low)


def dot(a, b, dims):
    return lax.dot_general(a, b, (dims, ((), ())), preferred_element_type=F32)


MESH = pl.DeviceIdType.MESH


def remote(source, goal, out, into, device):
    return pltpu.make_async_remote_copy(
        src_ref=source, dst_ref=goal, send_sem=out, recv_sem=into, device_id=device, device_id_type=MESH
    )


def wait(ref, sem):
    pltpu.make_async_copy(ref, ref, sem).wait()


def hail(device):
    pl.semaphore_signal(pltpu.get_barrier_semaphore(), inc=1, device_id=device, device_id_type=MESH)


def fir(taps, tile, weights, t0, store):
    step, rows = 8, weights[0].shape[0]
    tiles = [tile(i - (taps - 1)) for i in range(step + taps - 1)]
    for j in range(step):
        total = weights[0] * tiles[j + taps - 1]
        for m in range(1, taps):
            total += weights[m] * tiles[j + taps - 1 - m]
        store[pl.ds((t0 + j) * rows, rows), :] = total


def main_kernel(
    sides, planes, across, v_hbm, w_hbm, taps_hbm, high_hbm, low_hbm, order_ref, vis_hbm, got_ref,
    v_ref, w_ref, taps_ref, high_ref, low_ref, rim_ref, re_ref, im_ref, left_ref, right_ref, s_ref, x_ref, weights_ref,
    pick_ref, formed_ref, turned_ref, vis_ref, loads, saves, rim_send, rim_arrive, send, arrive, forward, forwarded, share, shared,
    beam_send, beam_arrive,
):
    owners = lax.axis_size("stn")
    pairs_count = owners // planes
    stn, beam = lax.axis_index("stn"), lax.axis_index("beam")
    p, place = stn // planes, stn % planes
    x, y = place // across, place % across
    side, core = beam // 2, beam % 2
    channels, quarters, _, stations, spectra = x_ref.shape
    rows = s_ref.shape[3]
    taps, points = taps_ref.shape
    mine, others = side * 2 + core, (1 - side) * 2 + core
    partner, sibling = (stn, others), (stn, side * 2 + 1 - core)
    later, sooner = (stn, (beam + 1) % quarters), (stn, (beam + quarters - 1) % quarters)
    near = (p + 3 + 2 * side) % pairs_count
    far = (p + 2) % pairs_count
    beyond = (p + 1 + 2 * side) % pairs_count
    nn, nt = ((1,), (0,)), ((1,), (1,))

    pieces = ((v_hbm, v_ref), (taps_hbm, taps_ref), (high_hbm, high_ref), (low_hbm, low_ref), (w_hbm, w_ref))
    fetches = [pltpu.make_async_copy(a, b, loads.at[i]) for i, (a, b) in enumerate(pieces)]
    for fetch in fetches:
        fetch.start()

    hail(sibling)
    hail(partner)
    hail(sooner)

    @pl.loop(1, owners)
    def _(i):
        hail(((stn + i) % owners, beam))

    @pl.loop(0, planes)
    def _(i):
        hail((near * planes + i, others))
        hail((far * planes + i, others))

    fetches[0].wait()
    fetches[1].wait()
    filters = [jnp.broadcast_to(taps_ref[m : m + 1, :], (rows, points)) for m in range(taps)]
    stores = (re_ref, im_ref)

    def inner(first, end):
        @pl.loop(first, end)
        def _(block):
            for part in range(2):

                def tile(i, part=part):
                    return v_ref[part, :, pl.ds(pl.multiple_of((block * 8 + i) * points, points), points)].astype(F32)

                fir(taps, tile, filters, block * 8, stores[part])

    blocks = spectra // 8
    inner(2, blocks // 2)
    pl.semaphore_wait(pltpu.get_barrier_semaphore(), owners - 1 + 2 * planes + 3)
    rim = (taps - 1) * points
    remote(v_ref.at[:, :, pl.ds((spectra - taps + 1) * points, rim)], rim_ref, rim_send, rim_arrive, later).start()

    inner(blocks // 2, blocks)
    wait(rim_ref, rim_arrive)
    for block in range(2):
        for part in range(2):

            def tile(i, block=block, part=part):
                t = block * 8 + i
                if t >= 0:
                    return v_ref[part, :, t * points : (t + 1) * points].astype(F32)
                t += taps - 1
                before = rim_ref[part, :, t * points : (t + 1) * points].astype(F32)
                return jnp.where(beam > 0, before, jnp.zeros_like(before))

            fir(taps, tile, filters, block * 8, stores[part])

    fetches[2].wait()
    fetches[3].wait()
    def transform(c):
        lines = 2 * owners
        cut = slice(c * lines, (c + 1) * lines)
        for i in range(rows):
            at = pl.ds(i, spectra, stride=rows)
            wide = jnp.concatenate([re_ref[at, :], im_ref[at, :]], axis=1)
            high = wide.astype(BF16)
            low = (wide - high.astype(F32)).astype(BF16)
            result = dot(high_ref[cut, :], high, nt) + dot(high_ref[cut, :], low, nt) + dot(low_ref[cut, :], high, nt)
            left_ref[pl.ds(c * lines * rows + i, lines, stride=rows), :] = result[:, :128]
            right_ref[pl.ds(c * lines * rows + i, lines, stride=rows), :] = result[:, 128:]

    def settle(c):
        @pl.loop(0, owners // 8)
        def _(i):
            count = 2 * rows
            for j in range(8):
                at = pl.ds(pl.multiple_of((c * owners + i * 8 + j) * count, count), count)
                s_ref[c, i * 8 + j, :, :, :128] = left_ref[at, :].astype(BF16).reshape(2, rows, 128)
                s_ref[c, i * 8 + j, :, :, 128:] = right_ref[at, :].astype(BF16).reshape(2, rows, 128)

    def entering(c, at, dx, groups):
        border = (p + 3 + 2 * at) % pairs_count
        for group in groups:
            pair, start = ((p, at), (border, at), (border, 1 - at), (far, 1 - at))[group]
            first = pl.multiple_of((pair * planes + ((x + across - dx) % across) * across) * rows, across * rows)
            yield group, x_ref.at[c, start * 2 + core, :, pl.ds(first, across * rows), :], start

    def landing(c):
        return x_ref.at[c, mine, :, pl.ds(pl.multiple_of(stn * rows, rows), rows), :]

    def stay(c):
        pltpu.make_async_copy(s_ref.at[c, stn], landing(c), arrive.at[c, 0, 0]).start()

    def depart(c, group, dx, dy):
        pair, entry = ((p, mine), (beyond, mine), (near, others), (far, others))[group]
        owner = pair * planes + ((x + dx) % across) * across + (y + dy) % across
        remote(s_ref.at[c, owner], landing(c), send.at[c], arrive.at[c, group, dx], (owner, entry)).start()

    def entered(c, groups, dx):
        for group, block, start in entering(c, side, dx, groups):
            wait(block, arrive.at[c, group, dx])
            remote(block, block, forward.at[c], forwarded.at[c, group, dx], partner).start()
            remote(block, block, share.at[c, start], shared.at[c, start], sibling).start()

    def passed(c, groups, dx):
        for group, block, start in entering(c, 1 - side, dx, groups):
            wait(block, forwarded.at[c, group, dx])
            remote(block, block, share.at[c, start], shared.at[c, start], sibling).start()

    half = w_ref.shape[2]

    def weigh(c):
        both = jnp.concatenate([w_ref[0, c], w_ref[1, c]], axis=0)
        for at in range(0, stations, 256):
            turned = dot(both, pick_ref[:, at : at + 256], nn)
            weights_ref[c, :, at : at + 256] = turned.astype(BF16)
            crossed = jnp.concatenate([-turned[half:], turned[:half]], axis=0)
            weights_ref[c, :, stations + at : stations + at + 256] = crossed.astype(BF16)

    def beams(c):
        for start in range(sides):
            wait(x_ref.at[c, start * 2 + 1 - core], shared.at[c, start])

        @pl.loop(0, quarters)
        def _(q):
            result = dot(weights_ref[c, :, :stations], x_ref[c, q, 0], nn)
            result += dot(weights_ref[c, :, stations:], x_ref[c, q, 1], nn)
            for part in range(2):
                formed = result[part * half : (part + 1) * half]
                left_ref[pl.ds(q * 2 + part, half, stride=8), :] = formed[:, :128]
                right_ref[pl.ds(q * 2 + part, half, stride=8), :] = formed[:, 128:]

        for d in range(0, owners, 8):
            at = slice(d * 16, (d + 8) * 16)
            formed_ref[c, d : d + 8, :, :128] = left_ref[at, :].astype(BF16).reshape(8, 16, 128)
            formed_ref[c, d : d + 8, :, 128:] = right_ref[at, :].astype(BF16).reshape(8, 16, 128)

        pltpu.make_async_copy(formed_ref.at[c, stn], got_ref.at[c, stn], beam_arrive.at[c]).start()

        def dispatch(owner):
            remote(formed_ref.at[c, owner], got_ref.at[c, stn], beam_send.at[c], beam_arrive.at[c], (owner, beam)).start()

        @pl.loop(0, planes)
        def _(i):
            for pair in (far, near, beyond):
                dispatch(pair * planes + (place + i) % planes)

            @pl.when(i > 0)
            def _():
                dispatch(p * planes + (place + i) % planes)

    count = vis_ref.shape[2]
    first_row = pl.multiple_of(beam * count, count)
    scale = 1.0 / (quarters * spectra)

    def arrange(c, some):
        for q in some:
            at = slice(q * spectra, (q + 1) * spectra)
            for part in range(2):
                for r in range(0, stations, 256):
                    turned_ref[part, r : r + 256, at] = dot(pick_ref[r : r + 256, :], x_ref[c, q, part], nn).astype(BF16)

    def correlate(c):
        real_rows = turned_ref[0, pl.ds(first_row, count), :]
        imag_rows = turned_ref[1, pl.ds(first_row, count), :]
        for at in range(0, stations, 256):
            cols = slice(at, at + 256)
            real, imag = turned_ref[0, cols, :], turned_ref[1, cols, :]
            vis_ref[0, c, :, cols] = (dot(real_rows, real, nt) + dot(imag_rows, imag, nt)) * scale
            vis_ref[1, c, :, cols] = (dot(imag_rows, real, nt) - dot(real_rows, imag, nt)) * scale
        pltpu.make_async_copy(vis_ref.at[:, c], vis_hbm.at[:, c], saves.at[c]).start()

    outer = (2, 1, 3)
    last = across - 1
    transform(0)
    settle(0)
    stay(0)

    @pl.loop(1, planes)
    def _(i):
        depart(0, 0, i // across, i % across)

    @pl.loop(0, planes)
    def _(i):
        for group in (3, 1, 2):
            depart(0, group, i // across, i % across)

    transform(1)
    settle(1)
    stay(1)

    def follow(dx):
        @pl.loop(0, across)
        def _(dy):
            for group in (3, 1, 2):
                depart(1, group, dx, dy)

    @pl.loop(1, planes)
    def _(i):
        depart(1, 0, i // across, i % across)

    follow(0)

    @pl.loop(0, across)
    def _(dx):
        entered(0, (0,), dx)

    @pl.loop(0, stations // 64)
    def _(i):
        first = pl.multiple_of(i * 64, 64)
        station = lax.broadcasted_iota(jnp.int32, (64, stations), 0) + first
        pick_ref[pl.ds(first, 64), :] = jnp.where(order_ref[...] == station, 1.0, 0.0).astype(BF16)

    fetches[4].wait()

    @pl.loop(0, across)
    def _(step):
        entered(0, outer, step)

        @pl.when(step < last)
        def _():
            follow(step + 1)

        @pl.when(step < channels)
        def _():
            weigh(step)

        passed(0, (0,), step)

        @pl.when(step > 0)
        def _():
            passed(0, outer, step - 1)

    @pl.loop(0, across)
    def _(dx):
        entered(1, (0,), dx)

    passed(0, outer, last)
    beams(0)
    entered(1, outer, 0)
    passed(1, (0,), 0)
    arrange(0, (0, 1))
    entered(1, outer, 1)
    passed(1, (0,), 1)
    passed(1, outer, 0)
    arrange(0, (2, 3))
    entered(1, outer, 2)
    passed(1, (0,), 2)
    passed(1, outer, 1)
    correlate(0)
    entered(1, outer, 3)
    passed(1, (0,), 3)
    passed(1, outer, 2)
    passed(1, outer, 3)
    beams(1)
    arrange(1, range(quarters))
    correlate(1)

    wait(rim_ref, rim_send)
    for c in range(channels):
        for start in range(sides):
            wait(x_ref.at[c, start * 2 + core], share.at[c, start])
        wait(x_ref.at[c, 0], forward.at[c])
        wait(s_ref.at[c, pl.ds(0, owners - 1)], send.at[c])
        wait(formed_ref.at[c, pl.ds(0, owners - 1)], beam_send.at[c])
        wait(vis_ref.at[:, c], saves.at[c])
        wait(got_ref.at[c], beam_arrive.at[c])


def main(voltages, beam_weights, filter_taps, station_order):
    quarters, owners = lax.axis_size("beam"), lax.axis_size("stn")
    taps, points = filter_taps.shape
    rows, spectra = voltages.shape[1], voltages.shape[2] // points
    channels, half, stations = beam_weights.shape[1:]
    across = 4
    order = np.arange(2 * points).reshape(2, owners, channels).transpose(2, 1, 0).reshape(-1)
    high, low = split(spin_matrix(points).T[order])
    dma = pltpu.SemaphoreType.DMA
    vmem, anywhere = pl.BlockSpec(memory_space=pltpu.VMEM), pl.BlockSpec(memory_space=pl.ANY)
    return pl.pallas_call(
        functools.partial(main_kernel, quarters // 2, across * across, across),
        out_shape=(
            jax.ShapeDtypeStruct((2, channels, stations // quarters, stations), F32),
            jax.ShapeDtypeStruct((channels, owners, 16, spectra), BF16),
        ),
        in_specs=[anywhere] * 5 + [vmem],
        out_specs=(anywhere, anywhere),
        scratch_shapes=[
            pltpu.VMEM(voltages.shape, BF16),
            pltpu.VMEM(beam_weights.shape, BF16),
            pltpu.VMEM(filter_taps.shape, F32),
            pltpu.VMEM(high.shape, BF16),
            pltpu.VMEM(low.shape, BF16),
            pltpu.VMEM((2, rows, (taps - 1) * points), BF16),
            pltpu.VMEM((spectra * rows, points), F32),
            pltpu.VMEM((spectra * rows, points), F32),
            pltpu.VMEM((2 * points * rows, 128), F32),
            pltpu.VMEM((2 * points * rows, 128), F32),
            pltpu.VMEM((channels, owners, 2, rows, spectra), BF16),
            pltpu.VMEM((channels, quarters, 2, stations, spectra), BF16),
            pltpu.VMEM((channels, 2 * half, 2 * stations), BF16),
            pltpu.VMEM((stations, stations), BF16),
            pltpu.VMEM((channels, owners, 16, spectra), BF16),
            pltpu.VMEM((2, stations, quarters * spectra), BF16),
            pltpu.VMEM((2, channels, stations // quarters, stations), F32),
            dma((5,)), dma((channels,)), dma, dma,
            dma((channels,)), dma((channels, 4, across)), dma((channels,)), dma((channels, 4, across)),
            dma((channels, 2)), dma((channels, 2)),
            dma((channels,)), dma((channels,)),
        ],
        compiler_params=pltpu.CompilerParams(collective_id=0, has_side_effects=True, vmem_limit_bytes=54 * MIB),
        name="main",
    )(voltages, beam_weights, filter_taps, high, low, station_order.reshape(1, stations))


def tail_kernel(
    taps, quarters, g_ref, vis_ref, taps_ref, high_ref, low_ref, out_hbm, kept_ref, held_ref, saved, out_ref, left_ref, right_ref, *lines
):
    pieces = [(i, c) for i in range(2) for c in range(vis_ref.shape[1])]
    fetches = [pltpu.make_async_copy(vis_ref.at[i], held_ref.at[i], saved.at[0, n]) for n, i in enumerate(pieces)]
    saves = [pltpu.make_async_copy(held_ref.at[i], kept_ref.at[i], saved.at[1, n]) for n, i in enumerate(pieces)]
    for fetch in fetches:
        fetch.start()
    channels = high_ref.shape[0] // 2
    spectra = g_ref.shape[1]
    pad = 16
    left_ref[...] = g_ref[:, :128].astype(F32)
    right_ref[...] = g_ref[:, 128:].astype(F32)
    tn = ((0,), (0,))
    for line in lines:
        line[:pad, :] = jnp.zeros((pad, channels), F32)
    for j in range(2):
        for q in range(quarters):
            parts = [
                jnp.concatenate(
                    [ref[pl.ds(j * 8 + q * 2 + ri, channels, stride=16), :] for ref in (left_ref, right_ref)], axis=1
                )
                for ri in range(2)
            ]
            both = jnp.concatenate(parts, axis=0).astype(BF16)
            result = dot(both, high_ref[...], tn) + dot(both, low_ref[...], tn)
            at = slice(pad + q * spectra, pad + (q + 1) * spectra)
            lines[2 * j][at, :] = result[:, :channels]
            lines[2 * j + 1][at, :] = result[:, channels:]
    for fetch, save in zip(fetches, saves):
        fetch.wait()
        save.start()
    block = 64
    weights = [jnp.broadcast_to(taps_ref[m : m + 1, :], (block, channels)) for m in range(taps)]
    leaving = [pltpu.make_async_copy(out_ref.at[part], out_hbm.at[part], saved.at[part, len(pieces)]) for part in range(2)]
    for part in range(2):
        for j in range(2):
            line = lines[2 * j + part]
            for t in range(0, quarters * spectra, block):
                total = weights[0] * line[pad + t : pad + t + block, :]
                for m in range(1, taps):
                    total += weights[m] * line[pad + t - m : pad + t - m + block, :]
                out_ref[part, pl.ds(2 * t + j, block, stride=2), :] = total
        leaving[part].start()
    for leave in leaving:
        leave.wait()
    for save in saves:
        save.wait()


def tail(arrived, visibilities, synth_taps, quarters, owners):
    taps, channels = synth_taps.shape
    rows, spectra = arrived.shape
    order = np.arange(2 * channels).reshape(2, owners, channels // owners).transpose(0, 2, 1).reshape(-1)
    high, low = split(spin_matrix(channels).T[order])
    vmem = pl.BlockSpec(memory_space=pltpu.VMEM)
    total = quarters * spectra
    return pl.pallas_call(
        functools.partial(tail_kernel, taps, quarters),
        out_shape=(
            jax.ShapeDtypeStruct((2, 2 * total, channels), F32),
            jax.ShapeDtypeStruct(visibilities.shape, F32),
        ),
        in_specs=[vmem, pl.BlockSpec(memory_space=pl.ANY), vmem, vmem, vmem],
        out_specs=(pl.BlockSpec(memory_space=pl.ANY),) * 2,
        scratch_shapes=[pltpu.VMEM(visibilities.shape, F32), pltpu.SemaphoreType.DMA((2, 5)), pltpu.VMEM((2, 2 * total, channels), F32)]
        + [pltpu.VMEM((rows, 128), F32)] * 2 + [pltpu.VMEM((total + 16, channels), F32)] * 4,
        compiler_params=pltpu.CompilerParams(vmem_limit_bytes=57 * MIB),
        name="tail",
    )(arrived, visibilities, synth_taps, high, low)


def local(voltages, filter_taps, synth_taps, beam_weights, station_order):
    quarters, owners = lax.axis_size("beam"), lax.axis_size("stn")
    channels = filter_taps.shape[1]
    spectra = voltages.shape[2] // channels
    visibilities, arrived = main(voltages, beam_weights, filter_taps, station_order)
    series, visibilities = tail(arrived.reshape(-1, spectra), visibilities, synth_taps, quarters, owners)
    series = series.reshape(2, quarters * spectra, 2, channels).transpose(0, 2, 1, 3)
    return visibilities, series.reshape(2, 1, 2, quarters * spectra * channels)


def solution(mesh):
    in_specs = (P(None, "stn", "beam"), P(), P(), P(None, "stn", "beam", None), P())
    out_specs = (P(None, "stn", "beam", None), P(None, "beam", "stn", None))
    return jax.shard_map(local, mesh=mesh, in_specs=in_specs, out_specs=out_specs, check_vma=False)
```
